512 devices in a mesh: segment: 4 (over x), dp: 8 (over y), mp: 16 (over z, core).
Axes of the slice: x: 4, y: 8, z: 8, core: 2. Of those that a mesh axis runs over, the one named last changes fastest.
Arguments:
- pending_inputs: bfloat16 [4, 8192, 4096], P('segment', ('dp', 'mp')), may hold values from -6 to 6
- arriving_samples: bfloat16 [8192, 4096], P(('dp', 'mp')), may hold values from -6 to 6
- layer_rms_gain: float32 [4, 4096], P('segment'), may hold values from 0.25 to 1.75
- scorer_vectors: float32 [4, 4096], P('segment'), may hold values from -0.09375 to 0.09375
- gating_matrix: bfloat16 [4, 4096, 14336], P('segment', 'dp', 'mp'), may hold values from -0.09375 to 0.09375
- expansion_matrix: bfloat16 [4, 4096, 14336], P('segment', 'dp', 'mp'), may hold values from -0.09375 to 0.09375
- contraction_matrix: bfloat16 [4, 14336, 4096], P('segment', 'mp', 'dp'), may hold values from -0.046875 to 0.046875
- dispatch_lists: int32 [2, 4, 128, 8], P(None, 'segment', ('dp', 'mp')), may hold values from -1 to 63, as said below
Outputs:
- first_out: bfloat16 [4, 8192, 4096], P('segment', ('dp', 'mp'))
- second_out: bfloat16 [4, 8192, 4096], P('segment', ('dp', 'mp'))
The draws below stay inside these ranges and needn't reach their ends.
Inputs may be any that keep to these rules, and one draw needn't show every extreme that they name: `dispatch_lists`: in each list of 8 slots the used slots come first and name distinct rows of the block; the other slots hold -1. Some block of every group of 8 blocks that share an mp index uses all 8 slots, and every such group (same tick and section) uses exactly 32 slots together.
All inputs are finite; a program needn't handle non-finite values.
Results may differ from the reference program's by a relative error of at most 0.0065.
Values may be sent and summed in bfloat16 or wider, within the bound.
No kernel may reach another device: no remote copies, remote signals or barrier semaphores. Data moves between devices by JAX's collectives and lax.ppermute only.
A program may use at most 64 MiB of HBM per device.

```python
import jax
import jax.numpy as jnp
from jax import lax

EMBED_DIM = 4096
FF = 14336
TOK_DEV = 64
TICKS = 2
CAP = 8
COLCAP = 32
SAMPLE_COUNT = 8192
N_SEGMENT = 4
N_DP = 8
N_MP = 16


def draw_dispatch_lists(key, part):
    key_amp = jax.random.fold_in(key, 11)
    key_order = jax.random.fold_in(key, 23)
    key_rows = jax.random.fold_in(key, 37)
    half = CAP // 2
    groups = TICKS * N_SEGMENT * N_MP
    amplitude = jax.random.randint(key_amp, (groups, N_DP // 2), 0, half + 1)
    amplitude = amplitude.at[:, 0].set(half)
    paired = jnp.concatenate([half + amplitude, half - amplitude], axis=1)
    order_keys = jax.random.split(key_order, groups)
    orders = jax.vmap(lambda sub_key: jax.random.permutation(sub_key, N_DP))(order_keys)
    counts = jnp.take_along_axis(paired, orders, axis=1)
    counts = counts.reshape(TICKS, N_SEGMENT, N_MP, N_DP)
    counts = jnp.transpose(counts, (0, 1, 3, 2)).reshape(TICKS, N_SEGMENT, N_DP * N_MP)
    row_keys = jax.random.split(key_rows, TICKS * N_SEGMENT * N_DP * N_MP)
    chosen = jax.vmap(lambda sub_key: jax.random.permutation(sub_key, TOK_DEV)[:CAP])(row_keys)
    chosen = chosen.reshape(TICKS, N_SEGMENT, N_DP * N_MP, CAP)
    slot_ids = jnp.arange(CAP, dtype=jnp.int32)
    return jnp.where(slot_ids < counts[..., None], chosen, -1).astype(jnp.int32)


def shard_levels(own_key, dims, cuts, least, largest):
    factor_of = 1.0
    for dim, parts in cuts:
        heights = jax.random.uniform(jax.random.fold_in(jax.random.fold_in(own_key, 6), dim), (parts,), jnp.float32, least / len(cuts), largest / len(cuts))
        factor_of = factor_of * jnp.repeat(jnp.exp(heights), dims[dim] // parts).reshape((-1,) + (1,) * (len(dims) - 1 - dim))
    return factor_of


def scatter_about(own_key, extent, scale, limit, cuts=(), held_as=jnp.bfloat16):
    level = shard_levels(own_key, extent, cuts, -0.22, 0.18) if cuts else 1.0
    array = jax.random.normal(own_key, extent, jnp.float32) * scale * level
    return jnp.minimum(jnp.maximum(array, -limit), limit).astype(held_as)


def setup_inputs(seed: int = 0) -> dict:
    keys = jax.random.split(jax.random.key(seed), 9)
    return {
        "pending_inputs": scatter_about(keys[0], (N_SEGMENT, SAMPLE_COUNT, EMBED_DIM), 1.0, 6.0, ((0, 4), (1, 128))),
        "arriving_samples": scatter_about(keys[1], (SAMPLE_COUNT, EMBED_DIM), 1.0, 6.0, ((0, 128),)),
        "layer_rms_gain": jnp.clip(1.0 + 0.15 * jax.random.normal(keys[2], (N_SEGMENT, EMBED_DIM), jnp.float32), 0.25, 1.75),
        "scorer_vectors": scatter_about(keys[3], (N_SEGMENT, EMBED_DIM), EMBED_DIM ** -0.5, 0.09375, ((0, 4),), jnp.float32),
        "gating_matrix": scatter_about(keys[4], (N_SEGMENT, EMBED_DIM, FF), EMBED_DIM ** -0.5, 0.09375, ((0, 4), (1, 8), (2, 16))),
        "expansion_matrix": scatter_about(keys[5], (N_SEGMENT, EMBED_DIM, FF), EMBED_DIM ** -0.5, 0.09375, ((0, 4), (1, 8), (2, 16))),
        "contraction_matrix": scatter_about(keys[6], (N_SEGMENT, FF, EMBED_DIM), FF ** -0.5, 0.046875, ((0, 4), (1, 16), (2, 8))),
        "dispatch_lists": draw_dispatch_lists(jax.random.fold_in(keys[8], 71), 0),
    }


def rounded(value):
    return lax.optimization_barrier(value.astype(jnp.bfloat16)).astype(jnp.float32)

def layer_tile(section_in, route_all, gain, router_vec, w_gate_sec, w_up_sec, w_down_sec):
    blocks = route_all.shape[0]
    block_base = (jnp.arange(blocks, dtype=jnp.int32) * TOK_DEV)[:, None]
    live_flat = (route_all >= 0).reshape(-1)
    row_flat = jnp.where(route_all >= 0, block_base + route_all, 0).reshape(-1).astype(jnp.int32)
    live_count = N_MP * COLCAP
    live_pos = jnp.nonzero(live_flat, size=live_count, fill_value=0)[0].astype(jnp.int32)
    row_index = jnp.take(row_flat, live_pos, axis=0).astype(jnp.int32)
    routed = jnp.take(section_in, row_index, axis=0).astype(jnp.float32)
    inv_rms = lax.rsqrt(lax.optimization_barrier(jnp.mean(routed * routed, axis=-1, keepdims=True)) + 1e-05)
    normed = (routed * inv_rms * gain).astype(jnp.bfloat16)
    feature_width = EMBED_DIM // N_DP
    gate = jnp.zeros((live_count, FF), jnp.float32)
    up_sum = jnp.zeros((live_count, FF), jnp.float32)
    for piece_index in range(N_DP):
        lower = piece_index * feature_width
        features = normed[:, lower:lower + feature_width]
        gate = gate + rounded(jnp.dot(features, w_gate_sec[lower:lower + feature_width], preferred_element_type=jnp.float32))
        up_sum = up_sum + rounded(jnp.dot(features, w_up_sec[lower:lower + feature_width], preferred_element_type=jnp.float32))
    hidden = (jax.nn.silu(gate) * up_sum).astype(jnp.bfloat16)
    unit_width = FF // N_MP
    block_out = jnp.zeros((live_count, EMBED_DIM), jnp.float32)
    for piece_index in range(N_MP):
        lower = piece_index * unit_width
        block_out = block_out + rounded(jnp.dot(hidden[:, lower:lower + unit_width], w_down_sec[lower:lower + unit_width], preferred_element_type=jnp.float32))
    block_out = rounded(block_out)
    weight = jax.nn.sigmoid(jnp.dot(routed, router_vec, precision=lax.Precision.HIGHEST))
    updated = (routed + weight[:, None] * block_out).astype(jnp.bfloat16)
    return section_in.at[row_index].set(updated)

def reference(pending_inputs, arriving_samples, layer_rms_gain, scorer_vectors, gating_matrix, expansion_matrix, contraction_matrix, dispatch_lists):
    front_entries = []
    for layer_number in range(N_SEGMENT):
        front_entries.append(layer_tile(pending_inputs[layer_number], dispatch_lists[0, layer_number], layer_rms_gain[layer_number], scorer_vectors[layer_number], gating_matrix[layer_number], expansion_matrix[layer_number], contraction_matrix[layer_number]))
    second_list = []
    for layer_number in range(N_SEGMENT):
        source = arriving_samples if layer_number == 0 else front_entries[layer_number - 1]
        second_list.append(layer_tile(source, dispatch_lists[1, layer_number], layer_rms_gain[layer_number], scorer_vectors[layer_number], gating_matrix[layer_number], expansion_matrix[layer_number], contraction_matrix[layer_number]))
    return (jnp.stack(front_entries), jnp.stack(second_list))
```

```python
import jax
import jax.numpy as jnp
from jax import lax
from jax.sharding import Mesh, PartitionSpec as P

BF = jnp.bfloat16
F32 = jnp.float32
DP = ("q", "h")
PLANE = ("h", "z")


def parts3(x):
    hi = x.astype(BF)
    r = x - hi.astype(F32)
    mid = r.astype(BF)
    lo = (r - mid.astype(F32)).astype(BF)
    return [hi, mid, lo]


def lanes(cols, n):
    at = jnp.arange(128, dtype=jnp.int32)[None, :]
    out = jnp.zeros((n, 128), BF)
    for i, col in enumerate(cols):
        out = jnp.where(at == i, col[:, None], out)
    return out


def compaction(live, rows):
    n = live.shape[0]
    i = jnp.arange(n, dtype=jnp.int32)
    place = jnp.sum(jnp.where((i[None, :] < i[:, None]) & live[None, :], 1, 0), axis=1)
    return ((place[None, :] == jnp.arange(rows, dtype=jnp.int32)[:, None]) & live[None, :]).astype(BF)


def pick(onehot, x):
    return jnp.dot(onehot, x, preferred_element_type=F32).astype(BF)


def cross(w):
    w = lax.ppermute(w, ("h", "core"), [(0, 0), (3, 3), (1, 2), (2, 1)])
    return w, lax.ppermute(w, "core", [(0, 1), (1, 0)])


def tick(v, gains, scorers, wg, wu, wd, z, core):
    rows = v.shape[0]
    n_z = lax.axis_size("z")
    n_q = lax.axis_size("q")
    width = v.shape[1]
    g = lax.all_to_all(
        jnp.broadcast_to(v[None], (2 * n_z, rows, width)), PLANE, 0, 0, tiled=True
    ).reshape(2, n_z * rows, width)
    ss = 0.0
    dot = 0.0
    gate = 0.0
    up = 0.0
    for k in range(2):
        vk = lax.dynamic_index_in_dim(g, core ^ k, 0, keepdims=False).astype(F32)
        ss = ss + jnp.sum(vk * vk, axis=1)
        dot = dot + jnp.sum(vk * scorers[k], axis=1)
        x = (vk * gains[k]).astype(BF)
        gate = gate + jnp.dot(x, wg[k], preferred_element_type=F32)
        up = up + jnp.dot(x, wu[k], preferred_element_type=F32)
    everyone = n_z * rows
    extra = lanes(parts3(ss) + parts3(dot), everyone)
    part = jnp.concatenate([gate.astype(BF), up.astype(BF), extra], axis=1)
    units = gate.shape[1]
    part = lax.all_to_all(part.reshape(n_q, everyone // n_q, -1), "q", 0, 0, tiled=True)
    total = jnp.sum(part.astype(F32), axis=0)
    ext = total[:, 2 * units :]
    inv = lax.rsqrt((ext[:, 0] + ext[:, 1] + ext[:, 2]) / (8 * width) + 1e-05)[:, None]
    weight = jax.nn.sigmoid(ext[:, 3] + ext[:, 4] + ext[:, 5])
    hidden = (jax.nn.silu(total[:, :units] * inv) * (total[:, units : 2 * units] * inv)).astype(BF)
    hidden = jnp.concatenate([hidden, lanes(parts3(weight), everyone // n_q)], axis=1)
    hidden = lax.all_gather(hidden, "q", axis=0, tiled=True)
    own = lax.dynamic_slice_in_dim(hidden[:, units:], z * rows, rows, 0).astype(F32)
    weight = own[:, 0] + own[:, 1] + own[:, 2]
    hidden = hidden[:, :units]
    outs = [jnp.dot(hidden, wd[k], preferred_element_type=F32).astype(BF) for k in range(2)]
    out = jnp.stack([jnp.where(core == 0, outs[0], outs[1]), jnp.where(core == 0, outs[1], outs[0])])
    out = lax.all_to_all(out.reshape(2 * n_z, rows, width), PLANE, 0, 0, tiled=True)
    block_out = jnp.sum(out.astype(F32), axis=0).astype(BF).astype(F32)
    return (v.astype(F32) + weight[:, None] * block_out).astype(BF)


def local(pending, arriving, gain, scorer, w_gate, w_up, w_down, lists):
    pending = pending[0]
    n_seg = lax.axis_size("segment")
    n_dp = lax.axis_size("q") * 2
    s = lax.axis_index("segment")
    q = lax.axis_index("q")
    z = lax.axis_index("z")
    core = lax.axis_index("core")
    n_rows, width = pending.shape
    cut = width // n_dp
    cap = lists.shape[-1]
    compact = n_dp * cap // 2
    e1 = lists[0, 0, 0]
    e2 = lists[1, 0, 0]
    e2_next = lax.ppermute(e2, "segment", [(i, (i - 1) % n_seg) for i in range(n_seg)])
    v1 = jnp.take(pending, jnp.maximum(e1, 0), axis=0)
    safe = jnp.maximum(e2_next, 0)
    b2 = jnp.where(s == n_seg - 1, jnp.take(arriving, safe, axis=0), jnp.take(pending, safe, axis=0))
    both = jnp.concatenate([v1, b2], axis=0).reshape(2 * cap, n_dp, cut).transpose(1, 0, 2)
    codes = lanes([jnp.concatenate([e1, e2_next]).astype(BF)], 2 * cap)
    both = jnp.concatenate([both, jnp.broadcast_to(codes[None], (n_dp, 2 * cap, 128))], axis=2)
    got = lax.all_to_all(both, DP, 0, 0, tiled=True)
    slots1 = got[:, :cap].reshape(n_dp * cap, -1)
    slots2 = got[:, cap:].reshape(n_dp * cap, -1)
    c1 = slots1[:, cut].astype(jnp.int32)
    c2 = slots2[:, cut].astype(jnp.int32)
    block = jnp.arange(n_dp * cap, dtype=jnp.int32) // cap
    comp1 = compaction(c1 >= 0, compact)
    comp2 = compaction(c2 >= 0, compact)
    same = (c2[:, None] == c1[None, :]) & (c1[None, :] >= 0) & (block[:, None] == block[None, :])
    same = (same & (s < n_seg - 1)).astype(BF)
    hit = pick(pick(comp2, same), comp1.T)
    has = jnp.sum(hit.astype(F32), axis=1)[:, None] > 0
    v1c = pick(comp1, slots1[:, :cut])
    b2c = pick(comp2, slots2[:, :cut])

    wg = cross(w_gate[0])
    wu = cross(w_up[0])
    wd = cross(w_down[0])

    def slices(row):
        return [lax.dynamic_slice_in_dim(row[0], (2 * q + (core ^ k)) * cut, cut, 0) for k in range(2)]

    gains, scorers = slices(gain), slices(scorer)
    up1 = tick(v1c, gains, scorers, wg, wu, wd, z, core)
    v2n = jnp.where(has, pick(hit, up1), b2c)
    ahead = [(i, (i + 1) % n_seg) for i in range(n_seg)]
    v2c = lax.ppermute(v2n, "segment", ahead)
    up1_slots = jnp.concatenate([pick(comp1.T, up1), slots1[:, cut:]], axis=1)
    comp2_slots = comp2.T
    before = lax.ppermute(
        jnp.concatenate([up1_slots, jnp.concatenate([comp2_slots, jnp.zeros((n_dp * cap, cut + 128 - compact), BF)], axis=1)], axis=0),
        "segment",
        ahead,
    )
    base = lax.ppermute(pending, "segment", ahead[:-1])
    up2 = tick(v2c, gains, scorers, wg, wu, wd, z, core)
    own_comp2 = before[n_dp * cap :, :compact]
    before = before[: n_dp * cap]
    up2_slots = jnp.concatenate([pick(own_comp2, up2), slots1[:, cut:]], axis=1)
    back = jnp.stack([x.reshape(n_dp, cap, -1) for x in (up1_slots, before, up2_slots)], axis=1)
    back = lax.all_to_all(back, DP, 0, 0, tiled=True)
    e1_before = back[0, 1, :, cut].astype(jnp.int32)
    rows = back[..., :cut].transpose(1, 2, 0, 3).reshape(3, cap, width)

    def put(into, at, new):
        return into.at[jnp.where(at >= 0, at, n_rows)].set(new, mode="drop")

    first = put(pending, e1, rows[0])
    second = jnp.where(s == 0, arriving, base)
    second = put(second, jnp.where(s == 0, -1, e1_before), rows[1])
    second = put(second, e2, rows[2])
    return first[None], second[None]


def solution(mesh):
    fine = Mesh(mesh.devices.reshape(4, 4, 2, 8, 2), ("segment", "q", "h", "z", "core"))
    dp, mp = ("q", "h"), ("z", "core")
    return jax.shard_map(
        local,
        mesh=fine,
        in_specs=(
            P("segment", dp + mp, None),
            P(dp + mp, None),
            P("segment", None),
            P("segment", None),
            P("segment", dp, mp),
            P("segment", dp, mp),
            P("segment", mp, dp),
            P(None, "segment", dp + mp, None),
        ),
        out_specs=(P("segment", dp + mp, None), P("segment", dp + mp, None)),
        check_vma=False,
    )
```

```python
import jax
import jax.numpy as jnp
from jax import lax
from jax.sharding import Mesh, PartitionSpec as P

BF = jnp.bfloat16
F32 = jnp.float32
DP = ("q", "h")
PLANE = ("h", "z")


def parts3(x):
    hi = x.astype(BF)
    r = x - hi.astype(F32)
    mid = r.astype(BF)
    lo = (r - mid.astype(F32)).astype(BF)
    return [hi, mid, lo]


def lanes(cols, n):
    at = jnp.arange(128, dtype=jnp.int32)[None, :]
    out = jnp.zeros((n, 128), BF)
    for i, col in enumerate(cols):
        out = jnp.where(at == i, col[:, None], out)
    return out


def compaction(live, rows):
    n = live.shape[0]
    i = jnp.arange(n, dtype=jnp.int32)
    place = jnp.sum(jnp.where((i[None, :] < i[:, None]) & live[None, :], 1, 0), axis=1)
    return ((place[None, :] == jnp.arange(rows, dtype=jnp.int32)[:, None]) & live[None, :]).astype(BF)


def pick(onehot, x):
    return jnp.dot(onehot, x, preferred_element_type=F32).astype(BF)


def cross(w):
    return lax.ppermute(w, ("h", "core"), [(0, 0), (3, 3), (1, 2), (2, 1)])


def sibling(w):
    return lax.ppermute(w, "core", [(0, 1), (1, 0)])


def after(x, *others):
    return lax.optimization_barrier((x, *others))


def tick(v, gains, scorers, w1, w2, base, z, core):
    rows = v.shape[0]
    n_z = lax.axis_size("z")
    n_q = lax.axis_size("q")
    width = v.shape[1]
    g = lax.all_to_all(
        jnp.broadcast_to(v[None], (2 * n_z, rows, width)), PLANE, 0, 0, tiled=True
    ).reshape(2, n_z * rows, width)
    g, *w1 = after(g, *w1)
    wg, wu = [w[0] for w in w1], [w[1] for w in w1]
    ss = 0.0
    dot = 0.0
    gate = 0.0
    up = 0.0
    for k in range(2):
        vk = lax.dynamic_index_in_dim(g, core ^ k, 0, keepdims=False).astype(F32)
        ss = ss + jnp.sum(vk * vk, axis=1)
        dot = dot + jnp.sum(vk * scorers[k], axis=1)
        x = (vk * gains[k]).astype(BF)
        gate = gate + jnp.dot(x, wg[k], preferred_element_type=F32)
        up = up + jnp.dot(x, wu[k], preferred_element_type=F32)
    everyone = n_z * rows
    extra = lanes(parts3(ss) + parts3(dot), everyone)
    part = jnp.concatenate([gate.astype(BF), up.astype(BF), extra], axis=1)
    units = gate.shape[1]
    part, w2_own = after(part, w2[0])
    part = lax.all_to_all(part.reshape(n_q, everyone // n_q, -1), "q", 0, 0, tiled=True)
    total = jnp.sum(part.astype(F32), axis=0)
    ext = total[:, 2 * units :]
    inv = lax.rsqrt((ext[:, 0] + ext[:, 1] + ext[:, 2]) / (8 * width) + 1e-05)[:, None]
    weight = jax.nn.sigmoid(ext[:, 3] + ext[:, 4] + ext[:, 5])
    hidden = (jax.nn.silu(total[:, :units] * inv) * (total[:, units : 2 * units] * inv)).astype(BF)
    hidden = jnp.concatenate([hidden, lanes(parts3(weight), everyone // n_q)], axis=1)
    hidden, w2_other = after(hidden, sibling(w2_own) if len(w2) == 1 else w2[1])
    wd = (w2_own, w2_other)
    hidden = lax.all_gather(hidden, "q", axis=0, tiled=True)
    own = lax.dynamic_slice_in_dim(hidden[:, units:], z * rows, rows, 0).astype(F32)
    weight = own[:, 0] + own[:, 1] + own[:, 2]
    hidden = hidden[:, :units]
    outs = [jnp.dot(hidden, wd[k], preferred_element_type=F32).astype(BF) for k in range(2)]
    out = jnp.stack([jnp.where(core == 0, outs[0], outs[1]), jnp.where(core == 0, outs[1], outs[0])])
    out, base = after(out, base)
    out = lax.all_to_all(out.reshape(2 * n_z, rows, width), PLANE, 0, 0, tiled=True)
    block_out = jnp.sum(out.astype(F32), axis=0).astype(BF).astype(F32)
    return (v.astype(F32) + weight[:, None] * block_out).astype(BF), wd, base


def local(pending, arriving, gain, scorer, w_gate, w_up, w_down, lists):
    pending = pending[0]
    n_seg = lax.axis_size("segment")
    n_dp = lax.axis_size("q") * 2
    s = lax.axis_index("segment")
    q = lax.axis_index("q")
    z = lax.axis_index("z")
    core = lax.axis_index("core")
    n_rows, width = pending.shape
    cut = width // n_dp
    cap = lists.shape[-1]
    compact = n_dp * cap // 2
    e1 = lists[0, 0, 0]
    e2 = lists[1, 0, 0]
    e2_next = lax.ppermute(e2, "segment", [(i, (i - 1) % n_seg) for i in range(n_seg)])
    v1 = jnp.take(pending, jnp.maximum(e1, 0), axis=0)
    safe = jnp.maximum(e2_next, 0)
    b2 = jnp.where(s == n_seg - 1, jnp.take(arriving, safe, axis=0), jnp.take(pending, safe, axis=0))
    both = jnp.concatenate([v1, b2], axis=0).reshape(2 * cap, n_dp, cut).transpose(1, 0, 2)
    codes = lanes([jnp.concatenate([e1, e2_next]).astype(BF)], 2 * cap)
    both = jnp.concatenate([both, jnp.broadcast_to(codes[None], (n_dp, 2 * cap, 128))], axis=2)
    got = lax.all_to_all(both, DP, 0, 0, tiled=True)
    slots1 = got[:, :cap].reshape(n_dp * cap, -1)
    slots2 = got[:, cap:].reshape(n_dp * cap, -1)
    c1 = slots1[:, cut].astype(jnp.int32)
    c2 = slots2[:, cut].astype(jnp.int32)
    block = jnp.arange(n_dp * cap, dtype=jnp.int32) // cap
    comp1 = compaction(c1 >= 0, compact)
    comp2 = compaction(c2 >= 0, compact)
    same = (c2[:, None] == c1[None, :]) & (c1[None, :] >= 0) & (block[:, None] == block[None, :])
    same = (same & (s < n_seg - 1)).astype(BF)
    hit = pick(pick(comp2, same), comp1.T)
    has = jnp.sum(hit.astype(F32), axis=1)[:, None] > 0
    v1c = pick(comp1, slots1[:, :cut])
    b2c = pick(comp2, slots2[:, :cut])

    w1 = cross(jnp.stack([w_gate[0], w_up[0]]))
    v1c, w1 = after(v1c, w1)
    w1 = (w1, sibling(w1))
    w2 = cross(w_down[0])
    ahead = [(i, (i + 1) % n_seg) for i in range(n_seg)]
    base = lax.ppermute(pending, "segment", ahead[:-1])

    def slices(row):
        return [lax.dynamic_slice_in_dim(row[0], (2 * q + (core ^ k)) * cut, cut, 0) for k in range(2)]

    gains, scorers = slices(gain), slices(scorer)
    up1, w2, base = tick(v1c, gains, scorers, w1, (w2,), base, z, core)
    v2n = jnp.where(has, pick(hit, up1), b2c)
    v2c = lax.ppermute(v2n, "segment", ahead)
    up1_slots = jnp.concatenate([pick(comp1.T, up1), slots1[:, cut:]], axis=1)
    comp2_slots = comp2.T
    before = lax.ppermute(
        jnp.concatenate([up1_slots, jnp.concatenate([comp2_slots, jnp.zeros((n_dp * cap, cut + 128 - compact), BF)], axis=1)], axis=0),
        "segment",
        ahead,
    )
    up2, _, base = tick(v2c, gains, scorers, w1, w2, base, z, core)
    own_comp2 = before[n_dp * cap :, :compact]
    before = before[: n_dp * cap]
    up2_slots = jnp.concatenate([pick(own_comp2, up2), slots1[:, cut:]], axis=1)
    back = jnp.stack([x.reshape(n_dp, cap, -1) for x in (up1_slots, before, up2_slots)], axis=1)
    back = lax.all_to_all(back, DP, 0, 0, tiled=True)
    e1_before = back[0, 1, :, cut].astype(jnp.int32)
    rows = back[..., :cut].transpose(1, 2, 0, 3).reshape(3, cap, width)

    def put(into, at, new):
        onehot = jnp.arange(n_rows, dtype=jnp.int32)[:, None] == at[None, :]
        return jnp.where(jnp.any(onehot, axis=1)[:, None], pick(onehot.astype(BF), new), into)

    first = put(pending, e1, rows[0])
    second = jnp.where(s == 0, arriving, base)
    replaced = jnp.any(e1_before[:, None] == jnp.where(e2 >= 0, e2, -2)[None, :], axis=1)
    e1_before = jnp.where((s == 0) | replaced, -1, e1_before)
    second = put(second, jnp.concatenate([e1_before, e2]), jnp.concatenate([rows[1], rows[2]], axis=0))
    return first[None], second[None]


def solution(mesh):
    fine = Mesh(mesh.devices.reshape(4, 4, 2, 8, 2), ("segment", "q", "h", "z", "core"))
    dp, mp = ("q", "h"), ("z", "core")
    return jax.shard_map(
        local,
        mesh=fine,
        in_specs=(
            P("segment", dp + mp, None),
            P(dp + mp, None),
            P("segment", None),
            P("segment", None),
            P("segment", dp, mp),
            P("segment", dp, mp),
            P("segment", mp, dp),
            P(None, "segment", dp + mp, None),
        ),
        out_specs=(P("segment", dp + mp, None), P("segment", dp + mp, None)),
        check_vma=False,
    )
```

```python
import jax
import jax.numpy as jnp
from jax import lax
from jax.sharding import Mesh, PartitionSpec as P

BF = jnp.bfloat16
F32 = jnp.float32
DP = ("q", "h")
PLANE = ("h", "z")


def parts3(x):
    hi = x.astype(BF)
    r = x - hi.astype(F32)
    mid = r.astype(BF)
    lo = (r - mid.astype(F32)).astype(BF)
    return [hi, mid, lo]


def lanes(cols, n):
    at = jnp.arange(128, dtype=jnp.int32)[None, :]
    out = jnp.zeros((n, 128), BF)
    for i, col in enumerate(cols):
        out = jnp.where(at == i, col[:, None], out)
    return out


def compaction(live, rows):
    n = live.shape[0]
    i = jnp.arange(n, dtype=jnp.int32)
    place = jnp.sum(jnp.where((i[None, :] < i[:, None]) & live[None, :], 1, 0), axis=1)
    return ((place[None, :] == jnp.arange(rows, dtype=jnp.int32)[:, None]) & live[None, :]).astype(BF)


def pick(onehot, x):
    return jnp.dot(onehot, x, preferred_element_type=F32).astype(BF)


def cross(w):
    return lax.ppermute(w, ("h", "core"), [(0, 0), (3, 3), (1, 2), (2, 1)])


def sibling(w):
    return lax.ppermute(w, "core", [(0, 1), (1, 0)])


def after(x, *others):
    return lax.optimization_barrier((x, *others))


def tick(v, gains, scorers, wg, wu, wd, late, z, core):
    rows, width = v.shape
    n_z = lax.axis_size("z")
    n_q = lax.axis_size("q")
    everyone = n_z * rows
    chunk = everyone // n_q
    g = lax.all_to_all(
        jnp.broadcast_to(v[None], (2 * n_z, rows, width)), PLANE, 0, 0, tiled=True
    ).reshape(2, everyone, width)
    ss = 0.0
    dot = 0.0
    gate = 0.0
    up = 0.0
    for k in range(2):
        vk = lax.dynamic_index_in_dim(g, core ^ k, 0, keepdims=False).astype(F32)
        ss = ss + jnp.sum(vk * vk, axis=1)
        dot = dot + jnp.sum(vk * scorers[k], axis=1)
        x = (vk * gains[k]).astype(BF)
        gate = gate + jnp.dot(x, wg[k], preferred_element_type=F32)
        up = up + jnp.dot(x, wu[k], preferred_element_type=F32)
    extra = lanes(parts3(ss) + parts3(dot), everyone)
    part = jnp.concatenate([gate.astype(BF), up.astype(BF), extra], axis=1)
    units = gate.shape[1]
    part, *late = after(part, *late)
    part = lax.all_to_all(part.reshape(n_q, chunk, -1), "q", 0, 0, tiled=True)
    total = jnp.sum(part.astype(F32), axis=0)
    ext = total[:, 2 * units :]
    inv = lax.rsqrt((ext[:, 0] + ext[:, 1] + ext[:, 2]) / (8 * width) + 1e-05)[:, None]
    weight = jax.nn.sigmoid(ext[:, 3] + ext[:, 4] + ext[:, 5])
    hidden = (jax.nn.silu(total[:, :units] * inv) * (total[:, units : 2 * units] * inv)).astype(BF)
    hidden = jnp.concatenate([hidden, lanes(parts3(weight), chunk)[:, :64]], axis=1)
    hidden = lax.all_gather(hidden, DP, axis=0, tiled=True).reshape(n_q, 2, chunk, -1)
    own = lax.dynamic_slice(hidden[:, 0, :, units:], (z * rows // chunk, z * rows % chunk, 0), (1, rows, 64))
    own = own[0].astype(F32)
    weight = own[:, 0] + own[:, 1] + own[:, 2]
    out = 0.0
    for k in range(2):
        hk = lax.dynamic_index_in_dim(hidden[..., :units], core ^ k, 1, keepdims=False)
        out = out + jnp.dot(hk.reshape(everyone, units), wd[k], preferred_element_type=F32)
    out = lax.all_to_all(out.astype(BF).reshape(n_z, rows, width), "z", 0, 0, tiled=True)
    block_out = jnp.sum(out.astype(F32), axis=0).astype(BF).astype(F32)
    return (v.astype(F32) + weight[:, None] * block_out).astype(BF), late


def local(pending, arriving, gain, scorer, w_gate, w_up, w_down, lists):
    pending = pending[0]
    n_seg = lax.axis_size("segment")
    n_dp = lax.axis_size("q") * 2
    s = lax.axis_index("segment")
    q = lax.axis_index("q")
    z = lax.axis_index("z")
    core = lax.axis_index("core")
    n_rows, width = pending.shape
    cut = width // n_dp
    cap = lists.shape[-1]
    compact = n_dp * cap // 2
    e1 = lists[0, 0, 0]
    e2 = lists[1, 0, 0]
    e2_next = lax.ppermute(e2, "segment", [(i, (i - 1) % n_seg) for i in range(n_seg)])
    v1 = jnp.take(pending, jnp.maximum(e1, 0), axis=0)
    safe = jnp.maximum(e2_next, 0)
    b2 = jnp.where(s == n_seg - 1, jnp.take(arriving, safe, axis=0), jnp.take(pending, safe, axis=0))
    both = jnp.concatenate([v1, b2], axis=0).reshape(2 * cap, n_dp, cut).transpose(1, 0, 2)
    codes = lanes([jnp.concatenate([e1, e2_next]).astype(BF)], 2 * cap)
    both = jnp.concatenate([both, jnp.broadcast_to(codes[None], (n_dp, 2 * cap, 128))], axis=2)
    both, wg = after(both, cross(w_gate[0]))
    got = lax.all_to_all(both, DP, 0, 0, tiled=True)
    slots1 = got[:, :cap].reshape(n_dp * cap, -1)
    slots2 = got[:, cap:].reshape(n_dp * cap, -1)
    c1 = slots1[:, cut].astype(jnp.int32)
    c2 = slots2[:, cut].astype(jnp.int32)
    block = jnp.arange(n_dp * cap, dtype=jnp.int32) // cap
    comp1 = compaction(c1 >= 0, compact)
    comp2 = compaction(c2 >= 0, compact)
    same = (c2[:, None] == c1[None, :]) & (c1[None, :] >= 0) & (block[:, None] == block[None, :])
    same = (same & (s < n_seg - 1)).astype(BF)
    hit = pick(pick(comp2, same), comp1.T)
    has = jnp.sum(hit.astype(F32), axis=1)[:, None] > 0
    v1c = pick(comp1, slots1[:, :cut])
    b2c = pick(comp2, slots2[:, :cut])

    v1c, wu = after(v1c, cross(w_up[0]))
    wg = (wg, sibling(wg))
    wu = (wu, sibling(wu))
    wd = (w_down[0], sibling(w_down[0]))
    ahead = [(i, (i + 1) % n_seg) for i in range(n_seg)]
    base = lax.ppermute(pending, "segment", ahead[:-1])

    def slices(row):
        return [lax.dynamic_slice_in_dim(row[0], (2 * q + (core ^ k)) * cut, cut, 0) for k in range(2)]

    gains, scorers = slices(gain), slices(scorer)
    up1, _ = tick(v1c, gains, scorers, wg, wu, wd, [], z, core)
    v2n = jnp.where(has, pick(hit, up1), b2c)
    v2c = lax.ppermute(v2n, "segment", ahead)
    up1_slots = jnp.concatenate([pick(comp1.T, up1), slots1[:, cut:]], axis=1)
    comp2_slots = comp2.T
    before = lax.ppermute(
        jnp.concatenate([up1_slots, jnp.concatenate([comp2_slots, jnp.zeros((n_dp * cap, cut + 128 - compact), BF)], axis=1)], axis=0),
        "segment",
        ahead,
    )
    up2, (before, base) = tick(v2c, gains, scorers, wg, wu, wd, [before, base], z, core)
    own_comp2 = before[n_dp * cap :, :compact]
    before = before[: n_dp * cap]
    up2_slots = jnp.concatenate([pick(own_comp2, up2), slots1[:, cut:]], axis=1)
    back = jnp.stack([x.reshape(n_dp, cap, -1) for x in (up1_slots, before, up2_slots)], axis=1)
    back = lax.all_to_all(back, DP, 0, 0, tiled=True)
    e1_before = back[0, 1, :, cut].astype(jnp.int32)
    rows = back[..., :cut].transpose(1, 2, 0, 3).reshape(3, cap, width)

    def put(into, at, new):
        onehot = jnp.arange(n_rows, dtype=jnp.int32)[:, None] == at[None, :]
        return jnp.where(jnp.any(onehot, axis=1)[:, None], pick(onehot.astype(BF), new), into)

    first = put(pending, e1, rows[0])
    second = jnp.where(s == 0, arriving, base)
    replaced = jnp.any(e1_before[:, None] == jnp.where(e2 >= 0, e2, -2)[None, :], axis=1)
    e1_before = jnp.where((s == 0) | replaced, -1, e1_before)
    second = put(second, jnp.concatenate([e1_before, e2]), jnp.concatenate([rows[1], rows[2]], axis=0))
    return first[None], second[None]


def solution(mesh):
    fine = Mesh(mesh.devices.reshape(4, 4, 2, 8, 2), ("segment", "q", "h", "z", "core"))
    dp, mp = ("q", "h"), ("z", "core")
    return jax.shard_map(
        local,
        mesh=fine,
        in_specs=(
            P("segment", dp + mp, None),
            P(dp + mp, None),
            P("segment", None),
            P("segment", None),
            P("segment", dp, mp),
            P("segment", dp, mp),
            P("segment", mp, dp),
            P(None, "segment", dp + mp, None),
        ),
        out_specs=(P("segment", dp + mp, None), P("segment", dp + mp, None)),
        check_vma=False,
    )
```

```python
import jax
import jax.numpy as jnp
from jax import lax
from jax.experimental import pallas as pl
from jax.experimental.pallas import tpu as pltpu
from jax.sharding import Mesh, PartitionSpec as P

BF = jnp.bfloat16
F32 = jnp.float32
DP = ("q", "h")
PLANE = ("h", "z")


def parts3(x):
    hi = x.astype(BF)
    r = x - hi.astype(F32)
    mid = r.astype(BF)
    lo = (r - mid.astype(F32)).astype(BF)
    return [hi, mid, lo]


def lanes(cols, n):
    at = jnp.arange(128, dtype=jnp.int32)[None, :]
    out = jnp.zeros((n, 128), BF)
    for i, col in enumerate(cols):
        out = jnp.where(at == i, col[:, None], out)
    return out


def compaction(live, rows):
    n = live.shape[0]
    i = jnp.arange(n, dtype=jnp.int32)
    place = jnp.sum(jnp.where((i[None, :] < i[:, None]) & live[None, :], 1, 0), axis=1)
    return ((place[None, :] == jnp.arange(rows, dtype=jnp.int32)[:, None]) & live[None, :]).astype(BF)


def pick(onehot, x):
    return jnp.dot(onehot, x, preferred_element_type=F32).astype(BF)


def cross(w):
    return lax.ppermute(w, ("h", "core"), [(0, 0), (3, 3), (1, 2), (2, 1)])


def sibling(w):
    return lax.ppermute(w, "core", [(0, 1), (1, 0)])


def after(x, *others):
    return lax.optimization_barrier((x, *others))


def project_body(core_ref, g_ref, gain_ref, scorer_ref, w0, w1, w2, w3, out_ref, held, sems):
    copies = [pltpu.make_async_copy(w, held.at[i], sems.at[i]) for i, w in enumerate((w0, w1, w2, w3))]
    for copy in copies:
        copy.start()
    core = core_ref[0]
    half = g_ref.shape[0] // 2
    width, units = w0.shape
    n = out_ref.shape[0]
    ss = jnp.zeros((n, 1), F32)
    dot = jnp.zeros((n, 1), F32)
    x = []
    for k in range(2):
        first = pl.multiple_of((core if k == 0 else 1 - core) * half, half)
        v = g_ref[pl.ds(first, half)].reshape(n, width).astype(F32)
        ss = ss + jnp.sum(v * v, axis=1, keepdims=True)
        dot = dot + jnp.sum(v * scorer_ref[k : k + 1, :], axis=1, keepdims=True)
        x.append((v * gain_ref[k : k + 1, :]).astype(BF))
    at = lax.broadcasted_iota(jnp.int32, (n, 128), 1)
    block = jnp.zeros((n, 128), F32)
    for i, col in enumerate(parts3(ss) + parts3(dot)):
        block = jnp.where(at == i, col.astype(F32), block)
    out_ref[:, 2 * units :] = block.astype(BF)
    for j in range(2):
        copies[2 * j].wait()
        total = jnp.dot(x[0], held[2 * j], preferred_element_type=F32)
        copies[2 * j + 1].wait()
        total = total + jnp.dot(x[1], held[2 * j + 1], preferred_element_type=F32)
        out_ref[:, j * units : (j + 1) * units] = total.astype(BF)


def project(g, gains, scorers, wg, wu, core):
    n = g.shape[0] // 2 * g.shape[1]
    width, units = wg[0].shape
    vmem = pl.BlockSpec(memory_space=pltpu.VMEM)
    anywhere = pl.BlockSpec(memory_space=pl.ANY)
    return pl.pallas_call(
        project_body,
        out_shape=jax.ShapeDtypeStruct((n, 2 * units + 128), BF),
        in_specs=[pl.BlockSpec(memory_space=pltpu.SMEM), vmem, vmem, vmem] + [anywhere] * 4,
        out_specs=vmem,
        scratch_shapes=[pltpu.VMEM((4, width, units), BF), pltpu.SemaphoreType.DMA((4,))],
        compiler_params=pltpu.CompilerParams(vmem_limit_bytes=40 * 2**20),
        cost_estimate=pl.CostEstimate(flops=8 * n * width * units, bytes_accessed=8 * width * units, transcendentals=0),
    )(jnp.reshape(core, (1,)).astype(jnp.int32), g, gains, scorers, wg[0], wg[1], wu[0], wu[1])


def tick(v, gains, scorers, wg, wu, wd, late, z, core):
    rows, width = v.shape
    n_z = lax.axis_size("z")
    n_q = lax.axis_size("q")
    everyone = n_z * rows
    chunk = everyone // n_q
    g = lax.all_to_all(
        jnp.broadcast_to(v[None], (2 * n_z, rows, width)), PLANE, 0, 0, tiled=True
    )
    part = project(g, gains, scorers, wg, wu, core)
    units = wg[0].shape[1]
    part, *late = after(part, *late)
    part = lax.all_to_all(part.reshape(n_q, chunk, -1), "q", 0, 0, tiled=True)
    total = jnp.sum(part.astype(F32), axis=0)
    ext = total[:, 2 * units :]
    inv = lax.rsqrt((ext[:, 0] + ext[:, 1] + ext[:, 2]) / (8 * width) + 1e-05)[:, None]
    weight = jax.nn.sigmoid(ext[:, 3] + ext[:, 4] + ext[:, 5])
    hidden = (jax.nn.silu(total[:, :units] * inv) * (total[:, units : 2 * units] * inv)).astype(BF)
    hidden = jnp.concatenate([hidden, lanes(parts3(weight), chunk)[:, :64]], axis=1)
    hidden = lax.all_gather(hidden, DP, axis=0, tiled=True).reshape(n_q, 2, chunk, -1)
    own = lax.dynamic_slice(hidden[:, 0, :, units:], (z * rows // chunk, z * rows % chunk, 0), (1, rows, 64))
    own = own[0].astype(F32)
    weight = own[:, 0] + own[:, 1] + own[:, 2]
    out = 0.0
    for k in range(2):
        hk = lax.dynamic_index_in_dim(hidden[..., :units], core ^ k, 1, keepdims=False)
        out = out + jnp.dot(hk.reshape(everyone, units), wd[k], preferred_element_type=F32)
    out = lax.all_to_all(out.astype(BF).reshape(n_z, rows, width), "z", 0, 0, tiled=True)
    block_out = jnp.sum(out.astype(F32), axis=0).astype(BF).astype(F32)
    return (v.astype(F32) + weight[:, None] * block_out).astype(BF), late


def local(pending, arriving, gain, scorer, w_gate, w_up, w_down, lists):
    pending = pending[0]
    n_seg = lax.axis_size("segment")
    n_dp = lax.axis_size("q") * 2
    s = lax.axis_index("segment")
    q = lax.axis_index("q")
    z = lax.axis_index("z")
    core = lax.axis_index("core")
    n_rows, width = pending.shape
    cut = width // n_dp
    cap = lists.shape[-1]
    compact = n_dp * cap // 2
    e1 = lists[0, 0, 0]
    e2 = lists[1, 0, 0]
    e2_next = lax.ppermute(e2, "segment", [(i, (i - 1) % n_seg) for i in range(n_seg)])
    at = jnp.arange(n_rows, dtype=jnp.int32)[None, :]
    wrap = s == n_seg - 1
    v1 = pick((e1[:, None] == at).astype(BF), pending)
    hit2 = e2_next[:, None] == at
    b2 = jnp.dot((hit2 & wrap).astype(BF), arriving, preferred_element_type=F32)
    b2 = (b2 + jnp.dot((hit2 & ~wrap).astype(BF), pending, preferred_element_type=F32)).astype(BF)
    both = jnp.concatenate([v1, b2], axis=0).reshape(2 * cap, n_dp, cut).transpose(1, 0, 2)
    codes = lanes([jnp.concatenate([e1, e2_next]).astype(BF)], 2 * cap)
    both = jnp.concatenate([both, jnp.broadcast_to(codes[None], (n_dp, 2 * cap, 128))], axis=2)
    both, w_g = after(both, w_gate[0])
    wg = cross(w_g)
    got = lax.all_to_all(both, DP, 0, 0, tiled=True)
    slots1 = got[:, :cap].reshape(n_dp * cap, -1)
    slots2 = got[:, cap:].reshape(n_dp * cap, -1)
    c1 = slots1[:, cut].astype(jnp.int32)
    c2 = slots2[:, cut].astype(jnp.int32)
    block = jnp.arange(n_dp * cap, dtype=jnp.int32) // cap
    comp1 = compaction(c1 >= 0, compact)
    comp2 = compaction(c2 >= 0, compact)
    same = (c2[:, None] == c1[None, :]) & (c1[None, :] >= 0) & (block[:, None] == block[None, :])
    same = (same & (s < n_seg - 1)).astype(BF)
    hit = pick(pick(comp2, same), comp1.T)
    has = jnp.sum(hit.astype(F32), axis=1)[:, None] > 0
    v1c = pick(comp1, slots1[:, :cut])
    b2c = pick(comp2, slots2[:, :cut])

    v1c, wg = after(v1c, wg)
    wu = cross(after(w_up[0], got)[0])
    wg = (wg, sibling(wg))
    wu = (wu, sibling(wu))
    wd = (w_down[0], sibling(w_down[0]))
    ahead = [(i, (i + 1) % n_seg) for i in range(n_seg)]
    base = lax.ppermute(pending, "segment", ahead[:-1])

    def slices(row):
        return jnp.stack([lax.dynamic_slice_in_dim(row[0], (2 * q + (core ^ k)) * cut, cut, 0) for k in range(2)])

    gains, scorers = slices(gain), slices(scorer)
    up1, _ = tick(v1c, gains, scorers, wg, wu, wd, [], z, core)
    v2n = jnp.where(has, pick(hit, up1), b2c)
    v2c = lax.ppermute(v2n, "segment", ahead)
    up1_slots = jnp.concatenate([pick(comp1.T, up1), slots1[:, cut:]], axis=1)
    comp2_slots = comp2.T
    before = lax.ppermute(
        jnp.concatenate([up1_slots, jnp.concatenate([comp2_slots, jnp.zeros((n_dp * cap, cut + 128 - compact), BF)], axis=1)], axis=0),
        "segment",
        ahead,
    )
    up2, (before, base) = tick(v2c, gains, scorers, wg, wu, wd, [before, base], z, core)
    own_comp2 = before[n_dp * cap :, :compact]
    before = before[: n_dp * cap]
    up2_slots = jnp.concatenate([pick(own_comp2, up2), slots1[:, cut:]], axis=1)
    back = jnp.stack([x.reshape(n_dp, cap, -1) for x in (up1_slots, before, up2_slots)], axis=1)
    back = lax.all_to_all(back, DP, 0, 0, tiled=True)
    e1_before = back[0, 1, :, cut].astype(jnp.int32)
    rows = back[..., :cut].transpose(1, 2, 0, 3).reshape(3, cap, width)

    def put(into, at, new):
        onehot = jnp.arange(n_rows, dtype=jnp.int32)[:, None] == at[None, :]
        return jnp.where(jnp.any(onehot, axis=1)[:, None], pick(onehot.astype(BF), new), into)

    first = put(pending, e1, rows[0])
    second = jnp.where(s == 0, arriving, base)
    replaced = jnp.any(e1_before[:, None] == jnp.where(e2 >= 0, e2, -2)[None, :], axis=1)
    e1_before = jnp.where((s == 0) | replaced, -1, e1_before)
    second = put(second, jnp.concatenate([e1_before, e2]), jnp.concatenate([rows[1], rows[2]], axis=0))
    return first[None], second[None]


def solution(mesh):
    fine = Mesh(mesh.devices.reshape(4, 4, 2, 8, 2), ("segment", "q", "h", "z", "core"))
    dp, mp = ("q", "h"), ("z", "core")
    return jax.shard_map(
        local,
        mesh=fine,
        in_specs=(
            P("segment", dp + mp, None),
            P(dp + mp, None),
            P("segment", None),
            P("segment", None),
            P("segment", dp, mp),
            P("segment", dp, mp),
            P("segment", mp, dp),
            P(None, "segment", dp + mp, None),
        ),
        out_specs=(P("segment", dp + mp, None), P("segment", dp + mp, None)),
        check_vma=False,
    )
```

```python
import functools

import jax
import jax.numpy as jnp
from jax import lax
from jax.experimental import pallas as pl
from jax.experimental.pallas import tpu as pltpu
from jax.sharding import Mesh, PartitionSpec as P

BF = jnp.bfloat16
F32 = jnp.float32
DP = ("q", "h")
PLANE = ("h", "z")


def parts3(x):
    hi = x.astype(BF)
    r = x - hi.astype(F32)
    mid = r.astype(BF)
    lo = (r - mid.astype(F32)).astype(BF)
    return [hi, mid, lo]


def lanes(cols, n):
    at = jnp.arange(128, dtype=jnp.int32)[None, :]
    out = jnp.zeros((n, 128), BF)
    for i, col in enumerate(cols):
        out = jnp.where(at == i, col[:, None], out)
    return out


def compaction(live, rows):
    n = live.shape[0]
    i = jnp.arange(n, dtype=jnp.int32)
    place = jnp.sum(jnp.where((i[None, :] < i[:, None]) & live[None, :], 1, 0), axis=1)
    return ((place[None, :] == jnp.arange(rows, dtype=jnp.int32)[:, None]) & live[None, :]).astype(BF)


def pick(onehot, x):
    return jnp.dot(onehot, x, preferred_element_type=F32).astype(BF)


def cross(w):
    return lax.ppermute(w, ("h", "core"), [(0, 0), (3, 3), (1, 2), (2, 1)])


def sibling(w):
    return lax.ppermute(w, "core", [(0, 1), (1, 0)])


def after(x, *others):
    return lax.optimization_barrier((x, *others))


def project_body(core_ref, g_ref, gain_ref, scorer_ref, w0, w1, w2, w3, out_ref, held, sems):
    copies = [pltpu.make_async_copy(w, held.at[i], sems.at[i]) for i, w in enumerate((w0, w1, w2, w3))]
    for copy in copies:
        copy.start()
    core = core_ref[0]
    half = g_ref.shape[0] // 2
    width, units = w0.shape
    n = out_ref.shape[0]
    ss = jnp.zeros((n, 1), F32)
    dot = jnp.zeros((n, 1), F32)
    x = []
    for k in range(2):
        first = pl.multiple_of((core if k == 0 else 1 - core) * half, half)
        v = g_ref[pl.ds(first, half)].reshape(n, width).astype(F32)
        ss = ss + jnp.sum(v * v, axis=1, keepdims=True)
        dot = dot + jnp.sum(v * scorer_ref[k : k + 1, :], axis=1, keepdims=True)
        x.append((v * gain_ref[k : k + 1, :]).astype(BF))
    at = lax.broadcasted_iota(jnp.int32, (n, 128), 1)
    block = jnp.zeros((n, 128), F32)
    for i, col in enumerate(parts3(ss) + parts3(dot)):
        block = jnp.where(at == i, col.astype(F32), block)
    out_ref[:, 2 * units :] = block.astype(BF)
    for j in range(2):
        copies[2 * j].wait()
        total = jnp.dot(x[0], held[2 * j], preferred_element_type=F32)
        copies[2 * j + 1].wait()
        total = total + jnp.dot(x[1], held[2 * j + 1], preferred_element_type=F32)
        out_ref[:, j * units : (j + 1) * units] = total.astype(BF)


def project(g, gains, scorers, wg, wu, core):
    n = g.shape[0] // 2 * g.shape[1]
    width, units = wg[0].shape
    vmem = pl.BlockSpec(memory_space=pltpu.VMEM)
    anywhere = pl.BlockSpec(memory_space=pl.ANY)
    return pl.pallas_call(
        project_body,
        out_shape=jax.ShapeDtypeStruct((n, 2 * units + 128), BF),
        in_specs=[pl.BlockSpec(memory_space=pltpu.SMEM), vmem, vmem, vmem] + [anywhere] * 4,
        out_specs=vmem,
        scratch_shapes=[pltpu.VMEM((4, width, units), BF), pltpu.SemaphoreType.DMA((4,))],
        compiler_params=pltpu.CompilerParams(vmem_limit_bytes=40 * 2**20),
        cost_estimate=pl.CostEstimate(flops=8 * n * width * units, bytes_accessed=8 * width * units, transcendentals=0),
    )(jnp.reshape(core, (1,)).astype(jnp.int32), g, gains, scorers, wg[0], wg[1], wu[0], wu[1])


def finish_body(features, part_ref, out_ref):
    chunk, lanes_out = out_ref.shape
    units = lanes_out - 64

    def summed(lo, n):
        total = part_ref[0, :, lo : lo + n].astype(F32)
        for i in range(1, part_ref.shape[0]):
            total = total + part_ref[i, :, lo : lo + n].astype(F32)
        return total

    ext = summed(2 * units, 128)
    inv = lax.rsqrt((ext[:, 0:1] + ext[:, 1:2] + ext[:, 2:3]) / features + 1e-05)
    weight = jax.nn.sigmoid(ext[:, 3:4] + ext[:, 4:5] + ext[:, 5:6])
    gate = summed(0, units) * inv
    out_ref[:, :units] = (jax.nn.silu(gate) * (summed(units, units) * inv)).astype(BF)
    at = lax.broadcasted_iota(jnp.int32, (chunk, 64), 1)
    block = jnp.zeros((chunk, 64), F32)
    for i, col in enumerate(parts3(weight)):
        block = jnp.where(at == i, col.astype(F32), block)
    out_ref[:, units:] = block.astype(BF)


def finish(part, units, features):
    vmem = pl.BlockSpec(memory_space=pltpu.VMEM)
    return pl.pallas_call(
        functools.partial(finish_body, features),
        out_shape=jax.ShapeDtypeStruct((part.shape[1], units + 64), BF),
        in_specs=[vmem],
        out_specs=vmem,
        compiler_params=pltpu.CompilerParams(vmem_limit_bytes=32 * 2**20),
        cost_estimate=pl.CostEstimate(flops=10 * part.size, bytes_accessed=2 * part.size, transcendentals=part.size // 8),
    )(part)


def lower_body(core_ref, hidden_ref, w0, w1, out_ref, held, sems):
    copies = [pltpu.make_async_copy(w, held.at[i], sems.at[i]) for i, w in enumerate((w0, w1))]
    for copy in copies:
        copy.start()
    core = core_ref[0]
    units = w0.shape[0]
    n = out_ref.shape[0]
    total = None
    for k in range(2):
        side = core if k == 0 else 1 - core
        x = hidden_ref[:, pl.ds(side, 1), :, :units].reshape(n, units)
        copies[k].wait()
        product = jnp.dot(x, held[k], preferred_element_type=F32)
        total = product if total is None else total + product
    out_ref[...] = total.astype(BF)


def lower(hidden, wd, core):
    n = hidden.shape[0] * hidden.shape[2]
    units, width = wd[0].shape
    vmem = pl.BlockSpec(memory_space=pltpu.VMEM)
    anywhere = pl.BlockSpec(memory_space=pl.ANY)
    return pl.pallas_call(
        lower_body,
        out_shape=jax.ShapeDtypeStruct((n, width), BF),
        in_specs=[pl.BlockSpec(memory_space=pltpu.SMEM), vmem, anywhere, anywhere],
        out_specs=vmem,
        scratch_shapes=[pltpu.VMEM((2, units, width), BF), pltpu.SemaphoreType.DMA((2,))],
        compiler_params=pltpu.CompilerParams(vmem_limit_bytes=32 * 2**20),
        cost_estimate=pl.CostEstimate(flops=4 * n * width * units, bytes_accessed=4 * width * units, transcendentals=0),
    )(jnp.reshape(core, (1,)).astype(jnp.int32), hidden, wd[0], wd[1])


def tick(v, gains, scorers, wg, wu, wd, late, z, core):
    rows, width = v.shape
    n_z = lax.axis_size("z")
    n_q = lax.axis_size("q")
    everyone = n_z * rows
    chunk = everyone // n_q
    g = lax.all_to_all(
        jnp.broadcast_to(v[None], (2 * n_z, rows, width)), PLANE, 0, 0, tiled=True
    )
    part = project(g, gains, scorers, wg, wu, core)
    units = wg[0].shape[1]
    part, *late = after(part, *late)
    part = lax.all_to_all(part.reshape(n_q, chunk, -1), "q", 0, 0, tiled=True)
    hidden = finish(part, units, 8 * width)
    hidden = lax.all_gather(hidden, DP, axis=0, tiled=True).reshape(n_q, 2, chunk, -1)
    own = lax.dynamic_slice(hidden[:, 0, :, units:], (z * rows // chunk, z * rows % chunk, 0), (1, rows, 64))
    own = own[0].astype(F32)
    weight = own[:, 0] + own[:, 1] + own[:, 2]
    out = lower(hidden, wd, core)
    out = lax.all_to_all(out.reshape(n_z, rows, width), "z", 0, 0, tiled=True)
    block_out = jnp.sum(out.astype(F32), axis=0).astype(BF).astype(F32)
    return (v.astype(F32) + weight[:, None] * block_out).astype(BF), late


def local(pending, arriving, gain, scorer, w_gate, w_up, w_down, lists):
    pending = pending[0]
    n_seg = lax.axis_size("segment")
    n_dp = lax.axis_size("q") * 2
    s = lax.axis_index("segment")
    q = lax.axis_index("q")
    z = lax.axis_index("z")
    core = lax.axis_index("core")
    n_rows, width = pending.shape
    cut = width // n_dp
    cap = lists.shape[-1]
    compact = n_dp * cap // 2
    e1 = lists[0, 0, 0]
    e2 = lists[1, 0, 0]
    e2_next = lax.ppermute(e2, "segment", [(i, (i - 1) % n_seg) for i in range(n_seg)])
    at = jnp.arange(n_rows, dtype=jnp.int32)[None, :]
    wrap = s == n_seg - 1
    v1 = pick((e1[:, None] == at).astype(BF), pending)
    hit2 = e2_next[:, None] == at
    b2 = jnp.dot((hit2 & wrap).astype(BF), arriving, preferred_element_type=F32)
    b2 = (b2 + jnp.dot((hit2 & ~wrap).astype(BF), pending, preferred_element_type=F32)).astype(BF)
    both = jnp.concatenate([v1, b2], axis=0).reshape(2 * cap, n_dp, cut).transpose(1, 0, 2)
    codes = lanes([jnp.concatenate([e1, e2_next]).astype(BF)], 2 * cap)
    both = jnp.concatenate([both, jnp.broadcast_to(codes[None], (n_dp, 2 * cap, 128))], axis=2)
    both, w_g = after(both, w_gate[0])
    wg = cross(w_g)
    got = lax.all_to_all(both, DP, 0, 0, tiled=True)
    slots1 = got[:, :cap].reshape(n_dp * cap, -1)
    slots2 = got[:, cap:].reshape(n_dp * cap, -1)
    c1 = slots1[:, cut].astype(jnp.int32)
    c2 = slots2[:, cut].astype(jnp.int32)
    block = jnp.arange(n_dp * cap, dtype=jnp.int32) // cap
    comp1 = compaction(c1 >= 0, compact)
    comp2 = compaction(c2 >= 0, compact)
    same = (c2[:, None] == c1[None, :]) & (c1[None, :] >= 0) & (block[:, None] == block[None, :])
    same = (same & (s < n_seg - 1)).astype(BF)
    hit = pick(pick(comp2, same), comp1.T)
    has = jnp.sum(hit.astype(F32), axis=1)[:, None] > 0
    v1c = pick(comp1, slots1[:, :cut])
    b2c = pick(comp2, slots2[:, :cut])

    v1c, wg = after(v1c, wg)
    wu = cross(after(w_up[0], got)[0])
    wg = (wg, sibling(wg))
    wu = (wu, sibling(wu))
    wd = (w_down[0], sibling(w_down[0]))
    ahead = [(i, (i + 1) % n_seg) for i in range(n_seg)]
    base = lax.ppermute(pending, "segment", ahead[:-1])

    def slices(row):
        return jnp.stack([lax.dynamic_slice_in_dim(row[0], (2 * q + (core ^ k)) * cut, cut, 0) for k in range(2)])

    gains, scorers = slices(gain), slices(scorer)
    up1, _ = tick(v1c, gains, scorers, wg, wu, wd, [], z, core)
    v2n = jnp.where(has, pick(hit, up1), b2c)
    v2c = lax.ppermute(v2n, "segment", ahead)
    up1_slots = jnp.concatenate([pick(comp1.T, up1), slots1[:, cut:]], axis=1)
    comp2_slots = comp2.T
    before = lax.ppermute(
        jnp.concatenate([up1_slots, jnp.concatenate([comp2_slots, jnp.zeros((n_dp * cap, cut + 128 - compact), BF)], axis=1)], axis=0),
        "segment",
        ahead,
    )
    up2, (before, base) = tick(v2c, gains, scorers, wg, wu, wd, [before, base], z, core)
    own_comp2 = before[n_dp * cap :, :compact]
    before = before[: n_dp * cap]
    up2_slots = jnp.concatenate([pick(own_comp2, up2), slots1[:, cut:]], axis=1)
    back = jnp.stack([x.reshape(n_dp, cap, -1) for x in (up1_slots, before, up2_slots)], axis=1)
    back = lax.all_to_all(back, DP, 0, 0, tiled=True)
    e1_before = back[0, 1, :, cut].astype(jnp.int32)
    rows = back[..., :cut].transpose(1, 2, 0, 3).reshape(3, cap, width)

    def put(into, at, new):
        onehot = jnp.arange(n_rows, dtype=jnp.int32)[:, None] == at[None, :]
        return jnp.where(jnp.any(onehot, axis=1)[:, None], pick(onehot.astype(BF), new), into)

    first = put(pending, e1, rows[0])
    second = jnp.where(s == 0, arriving, base)
    replaced = jnp.any(e1_before[:, None] == jnp.where(e2 >= 0, e2, -2)[None, :], axis=1)
    e1_before = jnp.where((s == 0) | replaced, -1, e1_before)
    second = put(second, jnp.concatenate([e1_before, e2]), jnp.concatenate([rows[1], rows[2]], axis=0))
    return first[None], second[None]


def solution(mesh):
    fine = Mesh(mesh.devices.reshape(4, 4, 2, 8, 2), ("segment", "q", "h", "z", "core"))
    dp, mp = ("q", "h"), ("z", "core")
    return jax.shard_map(
        local,
        mesh=fine,
        in_specs=(
            P("segment", dp + mp, None),
            P(dp + mp, None),
            P("segment", None),
            P("segment", None),
            P("segment", dp, mp),
            P("segment", dp, mp),
            P("segment", mp, dp),
            P(None, "segment", dp + mp, None),
        ),
        out_specs=(P("segment", dp + mp, None), P("segment", dp + mp, None)),
        check_vma=False,
    )
```

```python
import functools

import jax
import jax.numpy as jnp
from jax import lax
from jax.experimental import pallas as pl
from jax.experimental.pallas import tpu as pltpu
from jax.sharding import Mesh, PartitionSpec as P

BF = jnp.bfloat16
F32 = jnp.float32
DP = ("q", "h")
PLANE = ("h", "z")


def parts3(x):
    hi = x.astype(BF)
    r = x - hi.astype(F32)
    mid = r.astype(BF)
    lo = (r - mid.astype(F32)).astype(BF)
    return [hi, mid, lo]


def lanes(cols, n):
    at = jnp.arange(128, dtype=jnp.int32)[None, :]
    out = jnp.zeros((n, 128), BF)
    for i, col in enumerate(cols):
        out = jnp.where(at == i, col[:, None], out)
    return out


def compaction(live, rows):
    n = live.shape[0]
    i = jnp.arange(n, dtype=jnp.int32)
    place = jnp.sum(jnp.where((i[None, :] < i[:, None]) & live[None, :], 1, 0), axis=1)
    return ((place[None, :] == jnp.arange(rows, dtype=jnp.int32)[:, None]) & live[None, :]).astype(BF)


def pick(onehot, x):
    return jnp.dot(onehot, x, preferred_element_type=F32).astype(BF)


def cross(w):
    return lax.ppermute(w, ("h", "core"), [(0, 0), (3, 3), (1, 2), (2, 1)])


def sibling(w):
    return lax.ppermute(w, "core", [(0, 1), (1, 0)])


def after(x, *others):
    return lax.optimization_barrier((x, *others))


def project_body(core_ref, g_ref, gain_ref, scorer_ref, w0, w1, w2, w3, out_ref, held, sems):
    copies = [pltpu.make_async_copy(w, held.at[i], sems.at[i]) for i, w in enumerate((w0, w1, w2, w3))]
    for copy in copies:
        copy.start()
    core = core_ref[0]
    half = g_ref.shape[0] // 2
    width, units = w0.shape
    n = out_ref.shape[0]
    ss = jnp.zeros((n, 1), F32)
    dot = jnp.zeros((n, 1), F32)
    x = []
    for k in range(2):
        first = pl.multiple_of((core if k == 0 else 1 - core) * half, half)
        v = g_ref[pl.ds(first, half)].reshape(n, width).astype(F32)
        ss = ss + jnp.sum(v * v, axis=1, keepdims=True)
        dot = dot + jnp.sum(v * scorer_ref[k : k + 1, :], axis=1, keepdims=True)
        x.append((v * gain_ref[k : k + 1, :]).astype(BF))
    at = lax.broadcasted_iota(jnp.int32, (n, 128), 1)
    block = jnp.zeros((n, 128), F32)
    for i, col in enumerate(parts3(ss) + parts3(dot)):
        block = jnp.where(at == i, col.astype(F32), block)
    out_ref[:, 2 * units :] = block.astype(BF)
    for j in range(2):
        copies[2 * j].wait()
        total = jnp.dot(x[0], held[2 * j], preferred_element_type=F32)
        copies[2 * j + 1].wait()
        total = total + jnp.dot(x[1], held[2 * j + 1], preferred_element_type=F32)
        out_ref[:, j * units : (j + 1) * units] = total.astype(BF)


def project(g, gains, scorers, wg, wu, core):
    n = g.shape[0] // 2 * g.shape[1]
    width, units = wg[0].shape
    vmem = pl.BlockSpec(memory_space=pltpu.VMEM)
    anywhere = pl.BlockSpec(memory_space=pl.ANY)
    return pl.pallas_call(
        project_body,
        out_shape=jax.ShapeDtypeStruct((n, 2 * units + 128), BF),
        in_specs=[pl.BlockSpec(memory_space=pltpu.SMEM), vmem, vmem, vmem] + [anywhere] * 4,
        out_specs=vmem,
        scratch_shapes=[pltpu.VMEM((4, width, units), BF), pltpu.SemaphoreType.DMA((4,))],
        compiler_params=pltpu.CompilerParams(vmem_limit_bytes=40 * 2**20),
        cost_estimate=pl.CostEstimate(flops=8 * n * width * units, bytes_accessed=8 * width * units, transcendentals=0),
    )(jnp.reshape(core, (1,)).astype(jnp.int32), g, gains, scorers, wg[0], wg[1], wu[0], wu[1])


def finish_body(features, part_ref, out_ref):
    chunk, lanes_out = out_ref.shape
    units = lanes_out - 64

    def summed(lo, n):
        total = part_ref[0, :, lo : lo + n].astype(F32)
        for i in range(1, part_ref.shape[0]):
            total = total + part_ref[i, :, lo : lo + n].astype(F32)
        return total

    ext = summed(2 * units, 128)
    inv = lax.rsqrt((ext[:, 0:1] + ext[:, 1:2] + ext[:, 2:3]) / features + 1e-05)
    weight = jax.nn.sigmoid(ext[:, 3:4] + ext[:, 4:5] + ext[:, 5:6])
    gate = summed(0, units) * inv
    out_ref[:, :units] = (jax.nn.silu(gate) * (summed(units, units) * inv)).astype(BF)
    at = lax.broadcasted_iota(jnp.int32, (chunk, 64), 1)
    block = jnp.zeros((chunk, 64), F32)
    for i, col in enumerate(parts3(weight)):
        block = jnp.where(at == i, col.astype(F32), block)
    out_ref[:, units:] = block.astype(BF)


def finish(part, units, features):
    vmem = pl.BlockSpec(memory_space=pltpu.VMEM)
    return pl.pallas_call(
        functools.partial(finish_body, features),
        out_shape=jax.ShapeDtypeStruct((part.shape[1], units + 64), BF),
        in_specs=[vmem],
        out_specs=vmem,
        compiler_params=pltpu.CompilerParams(vmem_limit_bytes=32 * 2**20),
        cost_estimate=pl.CostEstimate(flops=10 * part.size, bytes_accessed=2 * part.size, transcendentals=part.size // 8),
    )(part)


def lower_body(core_ref, hidden_ref, w0, w1, out_ref, held, sems):
    copies = [pltpu.make_async_copy(w, held.at[i], sems.at[i]) for i, w in enumerate((w0, w1))]
    for copy in copies:
        copy.start()
    core = core_ref[0]
    units = w0.shape[0]
    n = out_ref.shape[0]
    total = None
    for k in range(2):
        side = core if k == 0 else 1 - core
        x = hidden_ref[:, pl.ds(side, 1), :, :units].reshape(n, units)
        copies[k].wait()
        product = jnp.dot(x, held[k], preferred_element_type=F32)
        total = product if total is None else total + product
    out_ref[...] = total.astype(BF)


def lower(hidden, wd, core):
    n = hidden.shape[0] * hidden.shape[2]
    units, width = wd[0].shape
    vmem = pl.BlockSpec(memory_space=pltpu.VMEM)
    anywhere = pl.BlockSpec(memory_space=pl.ANY)
    return pl.pallas_call(
        lower_body,
        out_shape=jax.ShapeDtypeStruct((n, width), BF),
        in_specs=[pl.BlockSpec(memory_space=pltpu.SMEM), vmem, anywhere, anywhere],
        out_specs=vmem,
        scratch_shapes=[pltpu.VMEM((2, units, width), BF), pltpu.SemaphoreType.DMA((2,))],
        compiler_params=pltpu.CompilerParams(vmem_limit_bytes=32 * 2**20),
        cost_estimate=pl.CostEstimate(flops=4 * n * width * units, bytes_accessed=4 * width * units, transcendentals=0),
    )(jnp.reshape(core, (1,)).astype(jnp.int32), hidden, wd[0], wd[1])


def tick(v, gains, scorers, wg, wu, wd, late, z, core):
    rows, width = v.shape
    n_z = lax.axis_size("z")
    n_q = lax.axis_size("q")
    everyone = n_z * rows
    chunk = everyone // n_q
    g = lax.all_to_all(
        jnp.broadcast_to(v[None], (2 * n_z, rows, width)), PLANE, 0, 0, tiled=True
    )
    part = project(g, gains, scorers, wg, wu, core)
    units = wg[0].shape[1]
    part, *late = after(part, *late)
    part = lax.all_to_all(part.reshape(n_q, chunk, -1), "q", 0, 0, tiled=True)
    hidden = finish(part, units, 8 * width)
    hidden = lax.all_gather(hidden, DP, axis=0, tiled=True).reshape(n_q, 2, chunk, -1)
    own = lax.dynamic_slice(hidden[:, 0, :, units:], (z * rows // chunk, z * rows % chunk, 0), (1, rows, 64))
    own = own[0].astype(F32)
    weight = own[:, 0] + own[:, 1] + own[:, 2]
    out = lower(hidden, wd, core)
    out = lax.all_to_all(out.reshape(n_z, rows, width), "z", 0, 0, tiled=True)
    block_out = jnp.sum(out.astype(F32), axis=0).astype(BF).astype(F32)
    return (v.astype(F32) + weight[:, None] * block_out).astype(BF), late


def local(pending, arriving, gain, scorer, w_gate, w_up, w_down, lists):
    pending = pending[0]
    n_seg = lax.axis_size("segment")
    n_dp = lax.axis_size("q") * 2
    s = lax.axis_index("segment")
    q = lax.axis_index("q")
    z = lax.axis_index("z")
    core = lax.axis_index("core")
    n_rows, width = pending.shape
    cut = width // n_dp
    cap = lists.shape[-1]
    compact = n_dp * cap // 2
    e1 = lists[0, 0, 0]
    e2 = lists[1, 0, 0]
    e2_next = lax.ppermute(e2, "segment", [(i, (i - 1) % n_seg) for i in range(n_seg)])
    at = jnp.arange(n_rows, dtype=jnp.int32)[None, :]
    wrap = s == n_seg - 1
    v1 = pick((e1[:, None] == at).astype(BF), pending)
    hit2 = e2_next[:, None] == at
    b2 = jnp.dot((hit2 & wrap).astype(BF), arriving, preferred_element_type=F32)
    b2 = (b2 + jnp.dot((hit2 & ~wrap).astype(BF), pending, preferred_element_type=F32)).astype(BF)
    both = jnp.concatenate([v1, b2], axis=0).reshape(2 * cap, n_dp, cut).transpose(1, 0, 2)
    codes = lanes([jnp.concatenate([e1, e2_next]).astype(BF)], 2 * cap)
    both = jnp.concatenate([both, jnp.broadcast_to(codes[None], (n_dp, 2 * cap, 128))], axis=2)
    both, w_g = after(both, w_gate[0])
    wg = cross(w_g)
    got = lax.all_to_all(both, DP, 0, 0, tiled=True)
    slots1 = got[:, :cap].reshape(n_dp * cap, -1)
    slots2 = got[:, cap:].reshape(n_dp * cap, -1)
    c1 = slots1[:, cut].astype(jnp.int32)
    c2 = slots2[:, cut].astype(jnp.int32)
    block = jnp.arange(n_dp * cap, dtype=jnp.int32) // cap
    comp1 = compaction(c1 >= 0, compact)
    comp2 = compaction(c2 >= 0, compact)
    same = (c2[:, None] == c1[None, :]) & (c1[None, :] >= 0) & (block[:, None] == block[None, :])
    same = (same & (s < n_seg - 1)).astype(BF)
    hit = pick(pick(comp2, same), comp1.T)
    has = jnp.sum(hit.astype(F32), axis=1)[:, None] > 0
    v1c = pick(comp1, slots1[:, :cut])
    b2c = pick(comp2, slots2[:, :cut])

    wu = cross(after(w_up[0], got)[0])
    wg = (wg, sibling(wg))
    wu = (wu, sibling(wu))
    wd = (w_down[0], sibling(w_down[0]))
    ahead = [(i, (i + 1) % n_seg) for i in range(n_seg)]
    base = lax.ppermute(pending, "segment", ahead[:-1])

    def slices(row):
        return jnp.stack([lax.dynamic_slice_in_dim(row[0], (2 * q + (core ^ k)) * cut, cut, 0) for k in range(2)])

    gains, scorers = slices(gain), slices(scorer)
    up1, _ = tick(v1c, gains, scorers, wg, wu, wd, [], z, core)
    v2n = jnp.where(has, pick(hit, up1), b2c)
    v2c = lax.ppermute(v2n, "segment", ahead)
    up1_slots = jnp.concatenate([pick(comp1.T, up1), slots1[:, cut:]], axis=1)
    comp2_slots = comp2.T
    before = lax.ppermute(
        jnp.concatenate([up1_slots, jnp.concatenate([comp2_slots, jnp.zeros((n_dp * cap, cut + 128 - compact), BF)], axis=1)], axis=0),
        "segment",
        ahead,
    )
    up2, (before, base) = tick(v2c, gains, scorers, wg, wu, wd, [before, base], z, core)
    own_comp2 = before[n_dp * cap :, :compact]
    before = before[: n_dp * cap]
    up2_slots = jnp.concatenate([pick(own_comp2, up2), slots1[:, cut:]], axis=1)
    back = jnp.stack([x.reshape(n_dp, cap, -1) for x in (up1_slots, before, up2_slots)], axis=1)
    back = lax.all_to_all(back, DP, 0, 0, tiled=True)
    e1_before = back[0, 1, :, cut].astype(jnp.int32)
    rows = back[..., :cut].transpose(1, 2, 0, 3).reshape(3, cap, width)

    def put(into, at, new):
        onehot = jnp.arange(n_rows, dtype=jnp.int32)[:, None] == at[None, :]
        return jnp.where(jnp.any(onehot, axis=1)[:, None], pick(onehot.astype(BF), new), into)

    first = put(pending, e1, rows[0])
    second = jnp.where(s == 0, arriving, base)
    replaced = jnp.any(e1_before[:, None] == jnp.where(e2 >= 0, e2, -2)[None, :], axis=1)
    e1_before = jnp.where((s == 0) | replaced, -1, e1_before)
    second = put(second, jnp.concatenate([e1_before, e2]), jnp.concatenate([rows[1], rows[2]], axis=0))
    return first[None], second[None]


def solution(mesh):
    fine = Mesh(mesh.devices.reshape(4, 4, 2, 8, 2), ("segment", "q", "h", "z", "core"))
    dp, mp = ("q", "h"), ("z", "core")
    return jax.shard_map(
        local,
        mesh=fine,
        in_specs=(
            P("segment", dp + mp, None),
            P(dp + mp, None),
            P("segment", None),
            P("segment", None),
            P("segment", dp, mp),
            P("segment", dp, mp),
            P("segment", mp, dp),
            P(None, "segment", dp + mp, None),
        ),
        out_specs=(P("segment", dp + mp, None), P("segment", dp + mp, None)),
        check_vma=False,
    )
```

```python
import functools

import jax
import jax.numpy as jnp
from jax import lax
from jax.experimental import pallas as pl
from jax.experimental.pallas import tpu as pltpu
from jax.sharding import Mesh, PartitionSpec as P

BF = jnp.bfloat16
F32 = jnp.float32
DP = ("q", "h")
PLANE = ("h", "z")


def parts3(x):
    hi = x.astype(BF)
    r = x - hi.astype(F32)
    mid = r.astype(BF)
    lo = (r - mid.astype(F32)).astype(BF)
    return [hi, mid, lo]


def lanes(cols, n):
    at = jnp.arange(128, dtype=jnp.int32)[None, :]
    out = jnp.zeros((n, 128), BF)
    for i, col in enumerate(cols):
        out = jnp.where(at == i, col[:, None], out)
    return out


def compaction(live, rows):
    n = live.shape[0]
    i = jnp.arange(n, dtype=jnp.int32)
    place = jnp.sum(jnp.where((i[None, :] < i[:, None]) & live[None, :], 1, 0), axis=1)
    return ((place[None, :] == jnp.arange(rows, dtype=jnp.int32)[:, None]) & live[None, :]).astype(BF)


def pick(onehot, x):
    return jnp.dot(onehot, x, preferred_element_type=F32).astype(BF)


def cross(w):
    return lax.ppermute(w, ("h", "core"), [(0, 0), (3, 3), (1, 2), (2, 1)])


def sibling(w):
    return lax.ppermute(w, "core", [(0, 1), (1, 0)])


def after(x, *others):
    return lax.optimization_barrier((x, *others))


def project_body(side_dim, core_ref, g_ref, gain_ref, scorer_ref, w0, w1, w2, w3, out_ref, held, sems):
    copies = [pltpu.make_async_copy(w, held.at[i], sems.at[i]) for i, w in enumerate((w0, w1, w2, w3))]
    for copy in copies:
        copy.start()
    core = core_ref[0]
    width, units = w0.shape
    n = out_ref.shape[0]
    ss = jnp.zeros((n, 1), F32)
    dot = jnp.zeros((n, 1), F32)
    x = []
    for k in range(2):
        side = pl.ds(core if k == 0 else 1 - core, 1)
        v = g_ref[side] if side_dim == 0 else g_ref[:, side]
        v = v.reshape(n, width).astype(F32)
        ss = ss + jnp.sum(v * v, axis=1, keepdims=True)
        dot = dot + jnp.sum(v * scorer_ref[k : k + 1, :], axis=1, keepdims=True)
        x.append((v * gain_ref[k : k + 1, :]).astype(BF))
    at = lax.broadcasted_iota(jnp.int32, (n, 128), 1)
    block = jnp.zeros((n, 128), F32)
    for i, col in enumerate(parts3(ss) + parts3(dot)):
        block = jnp.where(at == i, col.astype(F32), block)
    out_ref[:, 2 * units :] = block.astype(BF)
    for j in range(2):
        copies[2 * j].wait()
        total = jnp.dot(x[0], held[2 * j], preferred_element_type=F32)
        copies[2 * j + 1].wait()
        total = total + jnp.dot(x[1], held[2 * j + 1], preferred_element_type=F32)
        out_ref[:, j * units : (j + 1) * units] = total.astype(BF)


def project(g, side_dim, gains, scorers, wg, wu, core):
    n = g.shape[0] * g.shape[1] // 2 * g.shape[2]
    width, units = wg[0].shape
    vmem = pl.BlockSpec(memory_space=pltpu.VMEM)
    anywhere = pl.BlockSpec(memory_space=pl.ANY)
    return pl.pallas_call(
        functools.partial(project_body, side_dim),
        out_shape=jax.ShapeDtypeStruct((n, 2 * units + 128), BF),
        in_specs=[pl.BlockSpec(memory_space=pltpu.SMEM), vmem, vmem, vmem] + [anywhere] * 4,
        out_specs=vmem,
        scratch_shapes=[pltpu.VMEM((4, width, units), BF), pltpu.SemaphoreType.DMA((4,))],
        compiler_params=pltpu.CompilerParams(vmem_limit_bytes=40 * 2**20),
        cost_estimate=pl.CostEstimate(flops=8 * n * width * units, bytes_accessed=8 * width * units, transcendentals=0),
    )(jnp.reshape(core, (1,)).astype(jnp.int32), g, gains, scorers, wg[0], wg[1], wu[0], wu[1])


def finish_body(features, part_ref, out_ref):
    chunk, lanes_out = out_ref.shape
    units = lanes_out - 64

    def summed(lo, n):
        total = part_ref[0, :, lo : lo + n].astype(F32)
        for i in range(1, part_ref.shape[0]):
            total = total + part_ref[i, :, lo : lo + n].astype(F32)
        return total

    ext = summed(2 * units, 128)
    inv = lax.rsqrt((ext[:, 0:1] + ext[:, 1:2] + ext[:, 2:3]) / features + 1e-05)
    weight = jax.nn.sigmoid(ext[:, 3:4] + ext[:, 4:5] + ext[:, 5:6])
    gate = summed(0, units) * inv
    out_ref[:, :units] = (jax.nn.silu(gate) * (summed(units, units) * inv)).astype(BF)
    at = lax.broadcasted_iota(jnp.int32, (chunk, 64), 1)
    block = jnp.zeros((chunk, 64), F32)
    for i, col in enumerate(parts3(weight)):
        block = jnp.where(at == i, col.astype(F32), block)
    out_ref[:, units:] = block.astype(BF)


def finish(part, units, features):
    vmem = pl.BlockSpec(memory_space=pltpu.VMEM)
    return pl.pallas_call(
        functools.partial(finish_body, features),
        out_shape=jax.ShapeDtypeStruct((part.shape[1], units + 64), BF),
        in_specs=[vmem],
        out_specs=vmem,
        compiler_params=pltpu.CompilerParams(vmem_limit_bytes=32 * 2**20),
        cost_estimate=pl.CostEstimate(flops=10 * part.size, bytes_accessed=2 * part.size, transcendentals=part.size // 8),
    )(part)


def lower_body(core_ref, hidden_ref, w0, w1, out_ref, held, sems):
    copies = [pltpu.make_async_copy(w, held.at[i], sems.at[i]) for i, w in enumerate((w0, w1))]
    for copy in copies:
        copy.start()
    core = core_ref[0]
    units = w0.shape[0]
    n = out_ref.shape[0]
    total = None
    for k in range(2):
        side = core if k == 0 else 1 - core
        x = hidden_ref[:, pl.ds(side, 1), :, :units].reshape(n, units)
        copies[k].wait()
        product = jnp.dot(x, held[k], preferred_element_type=F32)
        total = product if total is None else total + product
    out_ref[...] = total.astype(BF)


def lower(hidden, wd, core):
    n = hidden.shape[0] * hidden.shape[2]
    units, width = wd[0].shape
    vmem = pl.BlockSpec(memory_space=pltpu.VMEM)
    anywhere = pl.BlockSpec(memory_space=pl.ANY)
    return pl.pallas_call(
        lower_body,
        out_shape=jax.ShapeDtypeStruct((n, width), BF),
        in_specs=[pl.BlockSpec(memory_space=pltpu.SMEM), vmem, anywhere, anywhere],
        out_specs=vmem,
        scratch_shapes=[pltpu.VMEM((2, units, width), BF), pltpu.SemaphoreType.DMA((2,))],
        compiler_params=pltpu.CompilerParams(vmem_limit_bytes=32 * 2**20),
        cost_estimate=pl.CostEstimate(flops=4 * n * width * units, bytes_accessed=4 * width * units, transcendentals=0),
    )(jnp.reshape(core, (1,)).astype(jnp.int32), hidden, wd[0], wd[1])


def tick(v, both, gains, scorers, wg, wu, wd, late, z, core):
    rows, width = v.shape
    n_z = lax.axis_size("z")
    n_q = lax.axis_size("q")
    everyone = n_z * rows
    chunk = everyone // n_q
    if both is None:
        g = lax.all_to_all(jnp.broadcast_to(v[None], (2 * n_z, rows, width)), PLANE, 0, 0, tiled=True)
        g, side_dim = g.reshape(2, n_z, rows, width), 0
    else:
        g = lax.all_to_all(jnp.broadcast_to(both[None], (n_z,) + both.shape), "z", 0, 0, tiled=True)
        side_dim = 1
    part = project(g, side_dim, gains, scorers, wg, wu, core)
    units = wg[0].shape[1]
    part, *late = after(part, *late)
    part = lax.all_to_all(part.reshape(n_q, chunk, -1), "q", 0, 0, tiled=True)
    hidden = finish(part, units, 8 * width)
    hidden = lax.all_gather(hidden, DP, axis=0, tiled=True).reshape(n_q, 2, chunk, -1)
    own = lax.dynamic_slice(hidden[:, 0, :, units:], (z * rows // chunk, z * rows % chunk, 0), (1, rows, 64))
    own = own[0].astype(F32)
    weight = own[:, 0] + own[:, 1] + own[:, 2]
    out = lower(hidden, wd, core)
    out = lax.all_to_all(out.reshape(n_z, rows, width), "z", 0, 0, tiled=True)
    block_out = jnp.sum(out.astype(F32), axis=0).astype(BF).astype(F32)
    return (v.astype(F32) + weight[:, None] * block_out).astype(BF), late


def local(pending, arriving, gain, scorer, w_gate, w_up, w_down, lists):
    pending = pending[0]
    n_seg = lax.axis_size("segment")
    n_dp = lax.axis_size("q") * 2
    s = lax.axis_index("segment")
    q = lax.axis_index("q")
    z = lax.axis_index("z")
    core = lax.axis_index("core")
    n_rows, width = pending.shape
    cut = width // n_dp
    cap = lists.shape[-1]
    compact = n_dp * cap // 2
    e1 = lists[0, 0, 0]
    e2 = lists[1, 0, 0]
    e2_next = lax.ppermute(e2, "segment", [(i, (i - 1) % n_seg) for i in range(n_seg)])
    at = jnp.arange(n_rows, dtype=jnp.int32)[None, :]
    wrap = s == n_seg - 1
    v1 = pick((e1[:, None] == at).astype(BF), pending)
    hit2 = e2_next[:, None] == at
    b2 = jnp.dot((hit2 & wrap).astype(BF), arriving, preferred_element_type=F32)
    b2 = (b2 + jnp.dot((hit2 & ~wrap).astype(BF), pending, preferred_element_type=F32)).astype(BF)
    pairs = v1.reshape(cap, n_dp // 2, 1, 2, cut).transpose(1, 2, 3, 0, 4)
    pairs = jnp.broadcast_to(pairs, (n_dp // 2, 2, 2, cap, cut)).reshape(n_dp, 2 * cap, cut)
    both = jnp.concatenate([pairs, b2.reshape(cap, n_dp, cut).transpose(1, 0, 2)], axis=1)
    codes = lanes([jnp.concatenate([e1, e1, e2_next]).astype(BF)], 3 * cap)
    both = jnp.concatenate([both, jnp.broadcast_to(codes[None], (n_dp, 3 * cap, 128))], axis=2)
    both, w_g, w_u = after(both, w_gate[0], w_up[0])
    wg = cross(w_g)
    wu = cross(w_u)
    got = lax.all_to_all(both, DP, 0, 0, tiled=True)
    slots1 = got[:, :cap].reshape(n_dp * cap, -1)
    far1 = got[:, cap : 2 * cap].reshape(n_dp * cap, -1)
    slots2 = got[:, 2 * cap :].reshape(n_dp * cap, -1)
    c1 = slots1[:, cut].astype(jnp.int32)
    c2 = slots2[:, cut].astype(jnp.int32)
    block = jnp.arange(n_dp * cap, dtype=jnp.int32) // cap
    comp1 = compaction(c1 >= 0, compact)
    comp2 = compaction(c2 >= 0, compact)
    same = (c2[:, None] == c1[None, :]) & (c1[None, :] >= 0) & (block[:, None] == block[None, :])
    same = (same & (s < n_seg - 1)).astype(BF)
    hit = pick(pick(comp2, same), comp1.T)
    has = jnp.sum(hit.astype(F32), axis=1)[:, None] > 0
    pair1 = jnp.stack([pick(comp1, slots1[:, :cut]), pick(comp1, far1[:, :cut])])
    v1c = jnp.where(lax.axis_index("h") == 0, pair1[0], pair1[1])
    b2c = pick(comp2, slots2[:, :cut])

    wg = (wg, sibling(wg))
    wu = (wu, sibling(wu))
    wd = (w_down[0], sibling(w_down[0]))
    ahead = [(i, (i + 1) % n_seg) for i in range(n_seg)]
    base = lax.ppermute(pending, "segment", ahead[:-1])

    def slices(row):
        return jnp.stack([lax.dynamic_slice_in_dim(row[0], (2 * q + (core ^ k)) * cut, cut, 0) for k in range(2)])

    gains, scorers = slices(gain), slices(scorer)
    up1, _ = tick(v1c, pair1, gains, scorers, wg, wu, wd, [], z, core)
    v2n = jnp.where(has, pick(hit, up1), b2c)
    v2c = lax.ppermute(v2n, "segment", ahead)
    up1_slots = jnp.concatenate([pick(comp1.T, up1), slots1[:, cut:]], axis=1)
    comp2_slots = comp2.T
    before = lax.ppermute(
        jnp.concatenate([up1_slots, jnp.concatenate([comp2_slots, jnp.zeros((n_dp * cap, cut + 128 - compact), BF)], axis=1)], axis=0),
        "segment",
        ahead,
    )
    up2, (before, base) = tick(v2c, None, gains, scorers, wg, wu, wd, [before, base], z, core)
    own_comp2 = before[n_dp * cap :, :compact]
    before = before[: n_dp * cap]
    up2_slots = jnp.concatenate([pick(own_comp2, up2), slots1[:, cut:]], axis=1)
    back = jnp.stack([x.reshape(n_dp, cap, -1) for x in (up1_slots, before, up2_slots)], axis=1)
    back = lax.all_to_all(back, DP, 0, 0, tiled=True)
    e1_before = back[0, 1, :, cut].astype(jnp.int32)
    rows = back[..., :cut].transpose(1, 2, 0, 3).reshape(3, cap, width)

    def put(into, at, new):
        onehot = jnp.arange(n_rows, dtype=jnp.int32)[:, None] == at[None, :]
        return jnp.where(jnp.any(onehot, axis=1)[:, None], pick(onehot.astype(BF), new), into)

    first = put(pending, e1, rows[0])
    second = jnp.where(s == 0, arriving, base)
    replaced = jnp.any(e1_before[:, None] == jnp.where(e2 >= 0, e2, -2)[None, :], axis=1)
    e1_before = jnp.where((s == 0) | replaced, -1, e1_before)
    second = put(second, jnp.concatenate([e1_before, e2]), jnp.concatenate([rows[1], rows[2]], axis=0))
    return first[None], second[None]


def solution(mesh):
    fine = Mesh(mesh.devices.reshape(4, 4, 2, 8, 2), ("segment", "q", "h", "z", "core"))
    dp, mp = ("q", "h"), ("z", "core")
    return jax.shard_map(
        local,
        mesh=fine,
        in_specs=(
            P("segment", dp + mp, None),
            P(dp + mp, None),
            P("segment", None),
            P("segment", None),
            P("segment", dp, mp),
            P("segment", dp, mp),
            P("segment", mp, dp),
            P(None, "segment", dp + mp, None),
        ),
        out_specs=(P("segment", dp + mp, None), P("segment", dp + mp, None)),
        check_vma=False,
    )
```

```python
import functools

import jax
import jax.numpy as jnp
from jax import lax
from jax.experimental import pallas as pl
from jax.experimental.pallas import tpu as pltpu
from jax.sharding import Mesh, PartitionSpec as P

BF = jnp.bfloat16
F32 = jnp.float32
DP = ("q", "h")
PLANE = ("h", "z")


def parts3(x):
    hi = x.astype(BF)
    r = x - hi.astype(F32)
    mid = r.astype(BF)
    lo = (r - mid.astype(F32)).astype(BF)
    return [hi, mid, lo]


def lanes(cols, n):
    at = jnp.arange(128, dtype=jnp.int32)[None, :]
    out = jnp.zeros((n, 128), BF)
    for i, col in enumerate(cols):
        out = jnp.where(at == i, col[:, None], out)
    return out


def compaction(live, rows):
    n = live.shape[0]
    i = jnp.arange(n, dtype=jnp.int32)
    place = jnp.sum(jnp.where((i[None, :] < i[:, None]) & live[None, :], 1, 0), axis=1)
    return ((place[None, :] == jnp.arange(rows, dtype=jnp.int32)[:, None]) & live[None, :]).astype(BF)


def pick(onehot, x):
    return jnp.dot(onehot, x, preferred_element_type=F32).astype(BF)


def cross(w):
    return lax.ppermute(w, ("h", "core"), [(0, 0), (3, 3), (1, 2), (2, 1)])


def sibling(w):
    return lax.ppermute(w, "core", [(0, 1), (1, 0)])


def after(x, *others):
    return lax.optimization_barrier((x, *others))


def project_body(side_dim, core_ref, g_ref, gain_ref, scorer_ref, w0, w1, w2, w3, out_ref, held, sems):
    copies = [pltpu.make_async_copy(w, held.at[i], sems.at[i]) for i, w in enumerate((w0, w1, w2, w3))]
    for copy in copies:
        copy.start()
    core = core_ref[0]
    width, units = w0.shape
    n = out_ref.shape[0]
    ss = jnp.zeros((n, 1), F32)
    dot = jnp.zeros((n, 1), F32)
    x = []
    for k in range(2):
        side = pl.ds(core if k == 0 else 1 - core, 1)
        v = g_ref[side] if side_dim == 0 else g_ref[:, side]
        v = v.reshape(n, width).astype(F32)
        ss = ss + jnp.sum(v * v, axis=1, keepdims=True)
        dot = dot + jnp.sum(v * scorer_ref[k : k + 1, :], axis=1, keepdims=True)
        x.append((v * gain_ref[k : k + 1, :]).astype(BF))
    at = lax.broadcasted_iota(jnp.int32, (n, 128), 1)
    block = jnp.zeros((n, 128), F32)
    for i, col in enumerate(parts3(ss) + parts3(dot)):
        block = jnp.where(at == i, col.astype(F32), block)
    out_ref[:, 2 * units :] = block.astype(BF)
    for j in range(2):
        copies[2 * j].wait()
        total = jnp.dot(x[0], held[2 * j], preferred_element_type=F32)
        copies[2 * j + 1].wait()
        total = total + jnp.dot(x[1], held[2 * j + 1], preferred_element_type=F32)
        out_ref[:, j * units : (j + 1) * units] = total.astype(BF)


def project(g, side_dim, gains, scorers, wg, wu, core):
    n = g.shape[0] * g.shape[1] // 2 * g.shape[2]
    width, units = wg[0].shape
    vmem = pl.BlockSpec(memory_space=pltpu.VMEM)
    anywhere = pl.BlockSpec(memory_space=pl.ANY)
    return pl.pallas_call(
        functools.partial(project_body, side_dim),
        out_shape=jax.ShapeDtypeStruct((n, 2 * units + 128), BF),
        in_specs=[pl.BlockSpec(memory_space=pltpu.SMEM), vmem, vmem, vmem] + [anywhere] * 4,
        out_specs=vmem,
        scratch_shapes=[pltpu.VMEM((4, width, units), BF), pltpu.SemaphoreType.DMA((4,))],
        compiler_params=pltpu.CompilerParams(vmem_limit_bytes=40 * 2**20),
        cost_estimate=pl.CostEstimate(flops=8 * n * width * units, bytes_accessed=8 * width * units, transcendentals=0),
    )(jnp.reshape(core, (1,)).astype(jnp.int32), g, gains, scorers, wg[0], wg[1], wu[0], wu[1])


def finish_body(features, part_ref, out_ref):
    chunk, lanes_out = out_ref.shape
    units = lanes_out - 64

    def summed(lo, n):
        total = part_ref[0, :, lo : lo + n].astype(F32)
        for i in range(1, part_ref.shape[0]):
            total = total + part_ref[i, :, lo : lo + n].astype(F32)
        return total

    ext = summed(2 * units, 128)
    inv = lax.rsqrt((ext[:, 0:1] + ext[:, 1:2] + ext[:, 2:3]) / features + 1e-05)
    weight = jax.nn.sigmoid(ext[:, 3:4] + ext[:, 4:5] + ext[:, 5:6])
    gate = summed(0, units) * inv
    out_ref[:, :units] = (jax.nn.silu(gate) * (summed(units, units) * inv)).astype(BF)
    at = lax.broadcasted_iota(jnp.int32, (chunk, 64), 1)
    block = jnp.zeros((chunk, 64), F32)
    for i, col in enumerate(parts3(weight)):
        block = jnp.where(at == i, col.astype(F32), block)
    out_ref[:, units:] = block.astype(BF)


def finish(part, units, features):
    vmem = pl.BlockSpec(memory_space=pltpu.VMEM)
    return pl.pallas_call(
        functools.partial(finish_body, features),
        out_shape=jax.ShapeDtypeStruct((part.shape[1], units + 64), BF),
        in_specs=[vmem],
        out_specs=vmem,
        compiler_params=pltpu.CompilerParams(vmem_limit_bytes=32 * 2**20),
        cost_estimate=pl.CostEstimate(flops=10 * part.size, bytes_accessed=2 * part.size, transcendentals=part.size // 8),
    )(part)


def lower_body(core_ref, hidden_ref, w0, w1, out_ref, held, sems):
    copies = [pltpu.make_async_copy(w, held.at[i], sems.at[i]) for i, w in enumerate((w0, w1))]
    for copy in copies:
        copy.start()
    core = core_ref[0]
    units = w0.shape[0]
    n = out_ref.shape[0]
    total = None
    for k in range(2):
        side = core if k == 0 else 1 - core
        x = hidden_ref[:, pl.ds(side, 1), :, :units].reshape(n, units)
        copies[k].wait()
        product = jnp.dot(x, held[k], preferred_element_type=F32)
        total = product if total is None else total + product
    out_ref[...] = total.astype(BF)


def lower(hidden, wd, core):
    n = hidden.shape[0] * hidden.shape[2]
    units, width = wd[0].shape
    vmem = pl.BlockSpec(memory_space=pltpu.VMEM)
    anywhere = pl.BlockSpec(memory_space=pl.ANY)
    return pl.pallas_call(
        lower_body,
        out_shape=jax.ShapeDtypeStruct((n, width), BF),
        in_specs=[pl.BlockSpec(memory_space=pltpu.SMEM), vmem, anywhere, anywhere],
        out_specs=vmem,
        scratch_shapes=[pltpu.VMEM((2, units, width), BF), pltpu.SemaphoreType.DMA((2,))],
        compiler_params=pltpu.CompilerParams(vmem_limit_bytes=32 * 2**20),
        cost_estimate=pl.CostEstimate(flops=4 * n * width * units, bytes_accessed=4 * width * units, transcendentals=0),
    )(jnp.reshape(core, (1,)).astype(jnp.int32), hidden, wd[0], wd[1])


def tick(v, both, gains, scorers, wg, wu, wd, late, z, core):
    rows, width = v.shape
    n_z = lax.axis_size("z")
    n_q = lax.axis_size("q")
    everyone = n_z * rows
    chunk = everyone // n_q
    if both is None:
        g = lax.all_to_all(jnp.broadcast_to(v[None], (2 * n_z, rows, width)), PLANE, 0, 0, tiled=True)
        g, side_dim = g.reshape(2, n_z, rows, width), 0
    else:
        g = lax.all_to_all(jnp.broadcast_to(both[None], (n_z,) + both.shape), "z", 0, 0, tiled=True)
        side_dim = 1
    part = project(g, side_dim, gains, scorers, wg, wu, core)
    units = wg[0].shape[1]
    part, *late = after(part, *late)
    part = lax.all_to_all(part.reshape(n_q, chunk, -1), "q", 0, 0, tiled=True)
    hidden = finish(part, units, 8 * width)
    hidden = lax.all_gather(hidden, DP, axis=0, tiled=True).reshape(n_q, 2, chunk, -1)
    own = lax.dynamic_slice(hidden[:, 0, :, units:], (z * rows // chunk, z * rows % chunk, 0), (1, rows, 64))
    own = own[0].astype(F32)
    weight = own[:, 0] + own[:, 1] + own[:, 2]
    out = lower(hidden, wd, core)
    out = lax.all_to_all(out.reshape(n_z, rows, width), "z", 0, 0, tiled=True)
    block_out = jnp.sum(out.astype(F32), axis=0).astype(BF).astype(F32)
    return (v.astype(F32) + weight[:, None] * block_out).astype(BF), late


def local(pending, arriving, gain, scorer, w_gate, w_up, w_down, lists):
    pending = pending[0]
    n_seg = lax.axis_size("segment")
    n_dp = lax.axis_size("q") * 2
    s = lax.axis_index("segment")
    q = lax.axis_index("q")
    z = lax.axis_index("z")
    core = lax.axis_index("core")
    n_rows, width = pending.shape
    cut = width // n_dp
    cap = lists.shape[-1]
    compact = n_dp * cap // 2
    e1 = lists[0, 0, 0]
    e2 = lists[1, 0, 0]
    e2_next = lax.ppermute(e2, "segment", [(i, (i - 1) % n_seg) for i in range(n_seg)])
    at = jnp.arange(n_rows, dtype=jnp.int32)[None, :]
    wrap = s == n_seg - 1
    v1 = pick((e1[:, None] == at).astype(BF), pending)
    hit2 = e2_next[:, None] == at
    b2 = jnp.dot((hit2 & wrap).astype(BF), arriving, preferred_element_type=F32)
    b2 = (b2 + jnp.dot((hit2 & ~wrap).astype(BF), pending, preferred_element_type=F32)).astype(BF)
    pairs = v1.reshape(cap, n_dp // 2, 1, 2, cut).transpose(1, 2, 3, 0, 4)
    pairs = jnp.broadcast_to(pairs, (n_dp // 2, 2, 2, cap, cut)).reshape(n_dp, 2 * cap, cut)
    both = jnp.concatenate([pairs, b2.reshape(cap, n_dp, cut).transpose(1, 0, 2)], axis=1)
    codes = lanes([jnp.concatenate([e1, e1, e2_next]).astype(BF)], 3 * cap)
    both = jnp.concatenate([both, jnp.broadcast_to(codes[None], (n_dp, 3 * cap, 128))], axis=2)
    both, w_g, w_u = after(both, w_gate[0], w_up[0])
    wg = cross(w_g)
    wu = cross(w_u)
    got = lax.all_to_all(both, DP, 0, 0, tiled=True)
    slots1 = got[:, :cap].reshape(n_dp * cap, -1)
    far1 = got[:, cap : 2 * cap].reshape(n_dp * cap, -1)
    slots2 = got[:, 2 * cap :].reshape(n_dp * cap, -1)
    c1 = slots1[:, cut].astype(jnp.int32)
    c2 = slots2[:, cut].astype(jnp.int32)
    block = jnp.arange(n_dp * cap, dtype=jnp.int32) // cap
    comp1 = compaction(c1 >= 0, compact)
    comp2 = compaction(c2 >= 0, compact)
    same = (c2[:, None] == c1[None, :]) & (c1[None, :] >= 0) & (block[:, None] == block[None, :])
    same = (same & (s < n_seg - 1)).astype(BF)
    hit = pick(pick(comp2, same), comp1.T)
    has = jnp.sum(hit.astype(F32), axis=1)[:, None] > 0
    pair1 = jnp.stack([pick(comp1, slots1[:, :cut]), pick(comp1, far1[:, :cut])])
    v1c = jnp.where(lax.axis_index("h") == 0, pair1[0], pair1[1])
    b2c = pick(comp2, slots2[:, :cut])

    wg = (wg, sibling(wg))
    wu = (wu, sibling(wu))
    wd = (w_down[0], sibling(w_down[0]))
    ahead = [(i, (i + 1) % n_seg) for i in range(n_seg)]
    base = lax.ppermute(pending, "segment", ahead[:-1])
    e1_before = lax.ppermute(e1, "segment", ahead)

    def slices(row):
        return jnp.stack([lax.dynamic_slice_in_dim(row[0], (2 * q + (core ^ k)) * cut, cut, 0) for k in range(2)])

    gains, scorers = slices(gain), slices(scorer)
    up1, _ = tick(v1c, pair1, gains, scorers, wg, wu, wd, [], z, core)
    v2n = jnp.where(has, pick(hit, up1), b2c)
    v2c = lax.ppermute(v2n, "segment", ahead)
    up1_slots = pick(comp1.T, up1)
    comp2_slots = comp2.T
    before = lax.ppermute(
        jnp.concatenate([up1_slots, jnp.concatenate([comp2_slots, jnp.zeros((n_dp * cap, cut - compact), BF)], axis=1)], axis=0),
        "segment",
        ahead,
    )
    up2, (before, base, e1_before) = tick(v2c, None, gains, scorers, wg, wu, wd, [before, base, e1_before], z, core)
    own_comp2 = before[n_dp * cap :, :compact]
    before = before[: n_dp * cap]
    up2_slots = pick(own_comp2, up2)
    back = jnp.stack([x.reshape(n_dp, cap, -1) for x in (up1_slots, before, up2_slots)], axis=1)
    back = lax.all_to_all(back, DP, 0, 0, tiled=True)
    rows = back.transpose(1, 2, 0, 3).reshape(3, cap, width)

    def put(into, at, new):
        onehot = jnp.arange(n_rows, dtype=jnp.int32)[:, None] == at[None, :]
        return jnp.where(jnp.any(onehot, axis=1)[:, None], pick(onehot.astype(BF), new), into)

    first = put(pending, e1, rows[0])
    second = jnp.where(s == 0, arriving, base)
    replaced = jnp.any(e1_before[:, None] == jnp.where(e2 >= 0, e2, -2)[None, :], axis=1)
    e1_before = jnp.where((s == 0) | replaced, -1, e1_before)
    second = put(second, jnp.concatenate([e1_before, e2]), jnp.concatenate([rows[1], rows[2]], axis=0))
    return first[None], second[None]


def solution(mesh):
    fine = Mesh(mesh.devices.reshape(4, 4, 2, 8, 2), ("segment", "q", "h", "z", "core"))
    dp, mp = ("q", "h"), ("z", "core")
    return jax.shard_map(
        local,
        mesh=fine,
        in_specs=(
            P("segment", dp + mp, None),
            P(dp + mp, None),
            P("segment", None),
            P("segment", None),
            P("segment", dp, mp),
            P("segment", dp, mp),
            P("segment", mp, dp),
            P(None, "segment", dp + mp, None),
        ),
        out_specs=(P("segment", dp + mp, None), P("segment", dp + mp, None)),
        check_vma=False,
    )
```
